32 devices in a mesh: groups: 2 (over x), ctx: 16 (over z, y, core).
Axes of the slice: x: 2, y: 2, z: 4, core: 2. Of those that a mesh axis runs over, the one named last changes fastest.
Arguments:
- queries: bfloat16 [4096, 2048], P(('groups', 'ctx')), parts along dimension 0, may hold values from -64 to 64
- keys: bfloat16 [4096, 512], P(('groups', 'ctx')), parts along dimension 0, may hold values from -6 to 6
- values: bfloat16 [4096, 512], P(('groups', 'ctx')), parts along dimension 0, may hold values from -6 to 6
- block_ids: int32 [4096], P(('groups', 'ctx')), parts along dimension 0, may hold values from 0 to 3, as said below
- out_weight: bfloat16 [2048, 2048], P('ctx'), may hold values from -0.59765625 to 0.59765625
- summary_gain: float32 [128], replicated, may hold values from 0.1 to 1.9
- norm_gain: float32 [2048], replicated, may hold values from 0.1 to 1.9
- routes: int32 [4096, 8], P(('groups', 'ctx')), parts along dimension 0, may hold values from 0 to 15, all different within a row; in each aligned block of 128 rows (0 to 127, 128 to 255, ...) at most 80 rows name the same one
- route_scores: float32 [4096, 8], P(('groups', 'ctx')), parts along dimension 0, may hold values from 0.02 to 1
- expert_gate: bfloat16 [16, 2048, 768], P('ctx'), may hold values from -0.125 to 0.125
- expert_up: bfloat16 [16, 2048, 768], P('ctx'), may hold values from -0.125 to 0.125
- expert_down: bfloat16 [16, 768, 2048], P('ctx'), may hold values from -0.21875 to 0.21875
Outputs:
- projected: bfloat16 [4096, 2048], P(('groups', 'ctx')), parts along dimension 0
- mixed: bfloat16 [4096, 2048], P(('groups', 'ctx')), parts along dimension 0
The draws below stay inside these ranges and needn't reach their ends.
There are 2 independent parts, one for each index of `groups`. The reference program is written for one: setup_inputs(seed, part) draws one part's arguments, and reference() takes and returns one part's arrays. A program takes and returns all parts, laid end to end along the dimension named above; an argument that names none is the same for every part. Nothing has to cross between parts.
Inputs may be any that keep to these rules, and one draw needn't show every extreme that they name: `block_ids`: within each context shard's 128 tokens the block numbers never fall, start at 0 and take every value up to 3. `routes`: among the 128 tokens of one context shard no expert is chosen more than 80 times, and in every draw some expert is chosen exactly 80 times by some shard. A token's 8 experts differ.
All inputs are finite; a program needn't handle non-finite values.
Results may differ from the reference program's by a relative error of at most 0.0077.
Values may be sent and summed in bfloat16 or wider, within the bound.
No kernel may reach another device: no remote copies, remote signals or barrier semaphores. Data moves between devices by JAX's collectives and lax.ppermute only.
A program may use at most 128 MiB of HBM per device.

```python
import math
import jax
import jax.numpy as jnp
import numpy as np
from jax import lax

D = 2048
HQ = 16
KVH = 4
HD = 128
FF = 768
TOP = 8
NB = 4
TOK_DEV = 128
TOKENS = 2048
EXPERTS = 16
CAP = 80


def query_key_pair(key):
    key_q = jax.random.fold_in(key, 101)
    key_k = jax.random.fold_in(key, 202)
    query = jax.random.truncated_normal(key_q, -6.0, 6.0, (TOKENS, HQ * HD), jnp.float32)
    keyed = jax.random.truncated_normal(key_k, -6.0, 6.0, (TOKENS, KVH * HD), jnp.float32)
    return (query, keyed)


def draw_queries(key, part):
    return query_key_pair(key)[0].astype(jnp.bfloat16)


def draw_keys(key, part):
    return query_key_pair(key)[1].astype(jnp.bfloat16)


def draw_block_ids(key, part):
    shards = TOKENS // TOK_DEV
    subkeys = jax.random.split(jax.random.fold_in(key, 303), shards)

    def one_shard(sub):
        cuts = jax.random.permutation(sub, TOK_DEV - 1)[:NB - 1] + 1
        position = jnp.arange(TOK_DEV)
        return jnp.sum((position[:, None] >= cuts[None, :]).astype(jnp.int32), axis=-1)
    return jax.vmap(one_shard)(subkeys).reshape(TOKENS).astype(jnp.int32)


def level_of(rng, shape, cuts, smallest, top_value):
    level = 1.0
    for dim, parts in cuts:
        heights = jax.random.uniform(jax.random.fold_in(jax.random.fold_in(rng, 6), dim), (parts,), jnp.float32, smallest / len(cuts), top_value / len(cuts))
        level = level * jnp.repeat(jnp.exp(heights), shape[dim] // parts).reshape((-1,) + (1,) * (len(shape) - 1 - dim))
    return level


def deal_out(stream_key, own, number, rows, number_of, top, most, slope):
    order = jax.random.permutation(stream_key, number_of)
    crowded, common = portions_of(number_of, rows * top, most, slope, True), portions_of(number_of, rows * top, most, slope, False)
    places = jnp.arange(number_of)

    def named(lengths, turn):
        used = int((lengths > 0).sum())
        fixed = max(1, used // 4)
        moved = fixed + (places - fixed + turn * (used - fixed)) % max(1, number_of - fixed)
        return jnp.zeros((number_of,), jnp.int32).at[order[jnp.where(places < fixed, places, moved)]].set(jnp.asarray(lengths, jnp.int32))

    lengths = jnp.where(number % 4 == 0, named(crowded, number // 4), named(common, number - number // 4 - 1))
    mixed = jax.random.permutation(jax.random.fold_in(own, 3), number_of)
    giver, sink = mixed[0:number_of // 2 * 2:2], mixed[1:number_of // 2 * 2:2]
    room = jnp.minimum(lengths[giver] - 1, most - lengths[sink]) // 2
    room = jnp.where((giver == order[0]) | (sink == order[0]) | (lengths[sink] == 0), 0, jnp.maximum(room, 0))
    moved = jax.random.randint(jax.random.fold_in(own, 4), (number_of // 2,), 0, 1 << 20) % (room + 1)
    lengths = lengths.at[giver].add(-moved).at[sink].add(moved)
    members = jnp.searchsorted(jnp.cumsum(lengths), jnp.arange(rows * top), side="right").astype(jnp.int32)
    listing = members.reshape(top, rows).T
    listing = listing[jax.random.permutation(jax.random.fold_in(own, 1), rows)]
    turn = jax.random.randint(jax.random.fold_in(own, 2), (rows, 1), 0, top)
    return jnp.take_along_axis(listing, (jnp.arange(top)[None, :] + turn) % top, axis=1)


def portions_of(count, total, limit, lean, full):
    portions = [(1 << 20) // math.isqrt(rank ** lean) + 1 for rank in range(1, count + 1)]
    largest = limit if full else min(limit, max(-(-total // count), total * portions[0] // sum(portions)))
    least = 1 if total - largest >= count - 1 else 0
    holding, spare = [largest] + [least] * (count - 1), total - largest - least * (count - 1)
    while spare > 0:
        free = [i for i in range(1, count) if holding[i] < largest] or [i for i in range(1, count) if holding[i] < limit]
        mass, budget = sum([portions[i] for i in free]), spare
        for i in free:
            more = min(limit - holding[i], max(1, budget * portions[i] // mass), spare)
            holding[i] = holding[i] + more
            spare = spare - more
    return np.array(holding)


def scatter_about(own_key, dims, spread, limit, pieces=(), held_as=jnp.bfloat16):
    array = jax.random.normal(own_key, dims, jnp.float32) * spread
    if len(pieces) > 0:
        array = level_of(own_key, dims, pieces, -0.22, 0.18) * array
    return jnp.clip(array, min=-limit, max=limit).astype(held_as)


def setup_inputs(seed: int = 0, part: int = 0) -> dict:
    seeds = jax.random.split(jax.random.key(seed), 13)
    part_splits = jax.random.split(jax.random.fold_in(seeds[12], part), 13)
    queries = draw_queries(jax.random.fold_in(jax.random.fold_in(seeds[12], part), 71), part)
    keys = draw_keys(jax.random.fold_in(jax.random.fold_in(seeds[12], part), 71), part)
    values = scatter_about(part_splits[2], (TOKENS, KVH * HD), 1.0, 6.0, ((0, 16),))
    block_ids = draw_block_ids(jax.random.fold_in(jax.random.fold_in(seeds[12], part), 71), part)
    out_weight = scatter_about(seeds[4], (HQ * HD, D), 0.1, 0.59765625, ((0, 16),))
    summary_gain = jnp.clip(1.0 + 0.18 * jax.random.normal(seeds[5], (HD,), jnp.float32), 0.1, 1.9)
    norm_gain = jnp.clip(1.0 + 0.18 * jax.random.normal(seeds[6], (D,), jnp.float32), 0.1, 1.9)
    routes_keys = jax.random.split(jax.random.fold_in(part_splits[7], 1), TOKENS // TOK_DEV)
    routes_turns = jax.random.permutation(jax.random.fold_in(part_splits[7], 3), TOKENS // TOK_DEV)
    routes = jax.vmap(lambda own, number: deal_out(jax.random.fold_in(part_splits[7], 2), own, number, TOK_DEV, EXPERTS, TOP, CAP, 2))(routes_keys, routes_turns).reshape((TOKENS, TOP))
    route_scores = jnp.clip(jnp.exp(math.log(1.0) - 3.912023 * jax.random.uniform(part_splits[8], (TOKENS, TOP), jnp.float32) ** level_of(part_splits[8], (TOKENS, TOP), ((0, 16),), -0.2, 0.2)), 0.02, 1.0)
    expert_gate = scatter_about(seeds[9], (EXPERTS, D, FF), D ** -0.5, 0.125, ((0, 16),))
    expert_up = scatter_about(seeds[10], (EXPERTS, D, FF), D ** -0.5, 0.125, ((0, 16),))
    expert_down = scatter_about(seeds[11], (EXPERTS, FF, D), FF ** -0.5, 0.21875, ((0, 16),))
    return {"queries": queries, "keys": keys, "values": values, "block_ids": block_ids, "out_weight": out_weight, "summary_gain": summary_gain, "norm_gain": norm_gain, "routes": routes, "route_scores": route_scores, "expert_gate": expert_gate, "expert_up": expert_up, "expert_down": expert_down}


def normalize(x):
    return x * lax.rsqrt(lax.optimization_barrier(jnp.mean(x * x, axis=-1, keepdims=True)) + 1e-06)

def reference(queries, keys, values, block_ids, out_weight, summary_gain, norm_gain, routes, route_scores, expert_gate, expert_up, expert_down):
    shards = TOKENS // TOK_DEV
    group = HQ // KVH
    scale = 1.0 / math.sqrt(HD)
    keys4 = keys.astype(jnp.float32).reshape(shards, TOK_DEV, KVH, HD)
    values4 = values.astype(jnp.float32).reshape(shards, TOK_DEV, KVH, HD)
    blocks = block_ids.reshape(shards, TOK_DEV)
    member = (blocks[:, None, :] == jnp.arange(NB, dtype=jnp.int32)[None, :, None]).astype(jnp.float32)
    count = lax.optimization_barrier(jnp.sum(member, axis=-1))
    kmean = jnp.einsum('nbt,ntkd->nbkd', member, keys4) / count[:, :, None, None]
    vmean = jnp.einsum('nbt,ntkd->nbkd', member, values4) / count[:, :, None, None]
    summary_keys = (normalize(kmean) * summary_gain.astype(jnp.float32)).astype(jnp.bfloat16).reshape(shards * NB, KVH, HD)
    summary_values = normalize(vmean).astype(jnp.bfloat16).reshape(shards * NB, KVH, HD)
    owner = jnp.arange(shards * NB, dtype=jnp.int32) // NB
    causal = jnp.arange(TOK_DEV)[:, None] >= jnp.arange(TOK_DEV)[None, :]

    def attend(index):
        start = (index * TOK_DEV).astype(jnp.int32)
        query = lax.dynamic_slice_in_dim(queries, start, TOK_DEV, 0).astype(jnp.float32).reshape(TOK_DEV, KVH, group, HD)
        key_loc = lax.dynamic_slice_in_dim(keys, start, TOK_DEV, 0).astype(jnp.float32).reshape(TOK_DEV, KVH, HD)
        val_loc = lax.dynamic_slice_in_dim(values, start, TOK_DEV, 0).reshape(TOK_DEV, KVH, HD)
        local = jnp.einsum('tkgd,skd->kgts', query, key_loc) * scale
        local = jnp.where(causal[None, None], local, -jnp.inf)
        remote = jnp.einsum('tkgd,skd->kgts', query, summary_keys.astype(jnp.float32)) * scale
        remote = jnp.where((owner < index)[None, None, None, :], remote, -jnp.inf)
        scores = jnp.concatenate([local, remote], axis=-1)
        top = lax.optimization_barrier(jnp.max(scores, axis=-1, keepdims=True))
        expo = jnp.exp(scores - top)
        weights = (expo / lax.optimization_barrier(jnp.sum(expo, axis=-1, keepdims=True))).astype(jnp.bfloat16)
        every_value = jnp.concatenate([val_loc, summary_values], axis=0)
        out = jnp.einsum('kgts,skd->tkgd', weights.astype(jnp.float32), every_value.astype(jnp.float32))
        return out.reshape(TOK_DEV, HQ * HD).astype(jnp.bfloat16)
    attended = lax.map(attend, jnp.arange(shards, dtype=jnp.int32)).reshape(TOKENS, HQ * HD)
    hidden = jnp.dot(attended, out_weight, preferred_element_type=jnp.float32)
    normed = (normalize(hidden) * norm_gain.astype(jnp.float32)).astype(jnp.bfloat16)
    combine = route_scores / lax.optimization_barrier(jnp.sum(route_scores, axis=-1, keepdims=True))
    slots = shards * CAP

    def expert_step(total, expert):
        picked = routes == expert
        weight_tok = lax.optimization_barrier(jnp.sum(jnp.where(picked, combine, 0.0), axis=-1))
        chosen = jnp.any(picked, axis=-1)
        rows = jnp.nonzero(chosen, size=slots, fill_value=0)[0].astype(jnp.int32)
        used = jnp.arange(slots) < jnp.sum(chosen.astype(jnp.int32))
        inputs = normed[rows]
        gate = jnp.dot(inputs, expert_gate[expert], preferred_element_type=jnp.float32)
        upper = jnp.dot(inputs, expert_up[expert], preferred_element_type=jnp.float32)
        act = (jax.nn.silu(gate) * upper).astype(jnp.bfloat16)
        result = jnp.dot(act, expert_down[expert], preferred_element_type=jnp.float32).astype(jnp.bfloat16)
        contrib = jnp.where(used[:, None], weight_tok[rows][:, None] * result.astype(jnp.float32), 0.0)
        return (total.at[rows].add(contrib), None)
    total, _ = lax.scan(expert_step, jnp.zeros((TOKENS, D), jnp.float32), jnp.arange(EXPERTS, dtype=jnp.int32))
    return (hidden.astype(jnp.bfloat16), (hidden + total).astype(jnp.bfloat16))
```

```python
import functools
import math

import jax
import jax.numpy as jnp
from jax import lax
from jax.experimental import pallas as pl
from jax.experimental.pallas import tpu as pltpu
from jax.sharding import PartitionSpec as P

D = 2048
HQ = 16
KVH = 4
HD = 128
TOP = 8
NB = 4
CORES = 2
VMEM_BYTES = 48 * 1024 * 1024
F32 = jnp.float32
BF16 = jnp.bfloat16


def normalize(x):
    return x * lax.rsqrt(jnp.mean(x * x, axis=-1, keepdims=True) + 1e-06)


def params():
    return pltpu.CompilerParams(vmem_limit_bytes=VMEM_BYTES)


def whole(*shape):
    return pl.BlockSpec(shape, lambda *_: (0,) * len(shape))


def summary_kernel(experts, ids, keys, values, gain, routes, scores, out, rows):
    tokens = ids.shape[1]
    block = lax.broadcasted_iota(jnp.int32, (8, tokens), 0)
    member = (ids[...] == block) & (block < NB)
    ones = jnp.where(member, 1.0, 0.0).astype(F32)
    count = jnp.maximum(jnp.sum(ones, axis=-1, keepdims=True), 1.0)
    indicator = ones.astype(BF16)
    kmean = jnp.dot(indicator, keys[...], preferred_element_type=F32) / count
    vmean = jnp.dot(indicator, values[...], preferred_element_type=F32) / count
    for g in range(KVH):
        cols = slice(g * HD, (g + 1) * HD)
        rows[8 * g : 8 * g + NB, :] = (normalize(kmean[:, cols]) * gain[...])[:NB]
        rows[8 * g + NB : 8 * g + 2 * NB, :] = normalize(vmean[:, cols])[:NB]
    base = 8 * KVH
    if experts:
        combine = scores[...] / jnp.sum(scores[...], axis=0, keepdims=True)
        expert = lax.broadcasted_iota(jnp.int32, (experts, tokens), 0)
        table = jnp.zeros((experts, tokens), F32)
        for k in range(TOP):
            table += jnp.where(routes[k : k + 1, :] == expert, combine[k : k + 1, :], 0.0)
        high = table.astype(BF16).astype(F32)
        rows[base : base + experts, :] = high
        rows[base + experts : base + 2 * experts, :] = table - high
    out[...] = rows[...].astype(BF16)


def summarize(ids, keys, values, gain, routes, scores, experts):
    tokens = ids.shape[0]
    height = 8 * KVH + 2 * experts
    return pl.pallas_call(
        functools.partial(summary_kernel, experts),
        out_shape=jax.ShapeDtypeStruct((height, HD), BF16),
        scratch_shapes=[pltpu.VMEM((height, HD), F32)],
        compiler_params=params(),
        name="summaries",
    )(ids.reshape(1, tokens), keys, values, gain.reshape(1, HD), routes.T, scores.T)


def attention_kernel(me, queries, keys, values, gathered, attended):
    tokens = queries.shape[0]
    group = HQ // KVH
    scale = 1.0 / math.sqrt(HD)
    shards = gathered.shape[0]
    wide = shards * 2 * NB
    row = lax.broadcasted_iota(jnp.int32, (tokens, tokens), 0)
    col = lax.broadcasted_iota(jnp.int32, (tokens, tokens), 1)
    causal = row >= col
    place = lax.broadcasted_iota(jnp.int32, (tokens, wide), 1)
    owner = (place // (2 * NB)) ^ me[1]
    earlier = (owner < me[0]) & (place % (2 * NB) < NB)
    seen = jnp.concatenate([causal, earlier], axis=1)
    for g in range(KVH):
        cols = slice(g * HD, (g + 1) * HD)
        pairs = gathered[:, 16 * (g // 2) : 16 * (g // 2) + 16, :].astype(F32)
        half = 8 * (g % 2)
        remote = pairs[:, half : half + 8, :].reshape(wide, HD)
        key_all = jnp.concatenate([keys[:, cols], remote.astype(BF16)], axis=0)
        shifted = pltpu.roll(remote, wide - NB, 0)
        value_all = jnp.concatenate([values[:, cols], shifted.astype(BF16)], axis=0)
        for i in range(group):
            h = g * group + i
            head = slice(h * HD, (h + 1) * HD)
            scores = (
                lax.dot_general(
                    queries[:, head],
                    key_all,
                    (((1,), (1,)), ((), ())),
                    preferred_element_type=F32,
                )
                * scale
            )
            scores = jnp.where(seen, scores, -jnp.inf)
            top = jnp.max(scores, axis=-1, keepdims=True)
            expo = jnp.exp(scores - top)
            weights = (expo / jnp.sum(expo, axis=-1, keepdims=True)).astype(BF16)
            attended[:, head] = jnp.dot(
                weights, value_all, preferred_element_type=F32
            ).astype(BF16)


def attend(me, queries, keys, values, gathered):
    tokens = queries.shape[0]
    return pl.pallas_call(
        attention_kernel,
        grid_spec=pltpu.PrefetchScalarGridSpec(
            num_scalar_prefetch=1,
            grid=(1,),
            in_specs=[whole(*a.shape) for a in (queries, keys, values, gathered)],
            out_specs=whole(tokens, HQ * HD),
        ),
        out_shape=jax.ShapeDtypeStruct((tokens, HQ * HD), BF16),
        compiler_params=params(),
        cost_estimate=pl.CostEstimate(
            flops=4 * HQ * HD * tokens * 2 * tokens,
            bytes_accessed=2 * 4 * tokens * HQ * HD,
            transcendentals=HQ * tokens * 2 * tokens,
        ),
        name="attention",
    )(me, queries, keys, values, gathered)


def project_first_kernel(chips, attended, *refs):
    blocks, acc, pair = refs[:-2], refs[-2], refs[-1]
    rows = blocks[0].shape[0]
    mine = chips[0]
    total = None
    for i in range(len(blocks) // 2):
        pair[pl.ds(pl.multiple_of(mine * rows, rows), rows), :] = blocks[2 * i][...]
        pair[pl.ds(pl.multiple_of((1 - mine) * rows, rows), rows), :] = blocks[2 * i + 1][...]
        at = pl.multiple_of(chips[i + 1] * 2 * rows, 2 * rows)
        part = jnp.dot(
            attended[:, pl.ds(at, 2 * rows)], pair[...], preferred_element_type=F32
        )
        if i == 0:
            acc[...] = part
        else:
            acc[...] += part


def project_first(chips, attended, blocks):
    tokens = attended.shape[0]
    rows, width = blocks[0].shape
    return pl.pallas_call(
        project_first_kernel,
        grid_spec=pltpu.PrefetchScalarGridSpec(
            num_scalar_prefetch=1,
            grid=(1,),
            in_specs=[whole(*attended.shape)] + [whole(rows, width)] * len(blocks),
            out_specs=whole(tokens, width),
            scratch_shapes=[pltpu.VMEM((2 * rows, width), BF16)],
        ),
        out_shape=jax.ShapeDtypeStruct((tokens, width), F32),
        compiler_params=params(),
        cost_estimate=pl.CostEstimate(
            flops=2 * tokens * rows * width * len(blocks),
            bytes_accessed=2 * rows * width * len(blocks),
            transcendentals=0,
        ),
        name="project_first",
    )(chips, attended, *blocks)


def project_last_kernel(chips, attended, acc, gain, a, b, c, d, hidden, projected, normed, pair):
    half = a.shape[0]
    rows = 2 * half
    mine = chips[0]
    own = pl.multiple_of(mine * rows, rows)
    other = pl.multiple_of((1 - mine) * rows, rows)
    pair[pl.ds(own, half), :] = a[...]
    pair[pl.ds(own + half, half), :] = b[...]
    pair[pl.ds(other, half), :] = c[...]
    pair[pl.ds(other + half, half), :] = d[...]
    at = pl.multiple_of(chips[1] * 2 * rows, 2 * rows)
    total = acc[...] + jnp.dot(
        attended[:, pl.ds(at, 2 * rows)], pair[...], preferred_element_type=F32
    )
    hidden[...] = total
    projected[...] = total.astype(BF16)
    normed[...] = (normalize(total) * gain[...]).astype(BF16)


def project_last(chips, attended, acc, gain, halves):
    tokens, width = acc.shape
    half = halves[0].shape[0]
    return pl.pallas_call(
        project_last_kernel,
        grid_spec=pltpu.PrefetchScalarGridSpec(
            num_scalar_prefetch=1,
            grid=(1,),
            in_specs=[whole(*attended.shape), whole(tokens, width), whole(1, width)]
            + [whole(half, width)] * 4,
            out_specs=[whole(tokens, width)] * 3,
            scratch_shapes=[pltpu.VMEM((4 * half, width), BF16)],
        ),
        out_shape=[
            jax.ShapeDtypeStruct((tokens, width), F32),
            jax.ShapeDtypeStruct((tokens, width), BF16),
            jax.ShapeDtypeStruct((tokens, width), BF16),
        ],
        compiler_params=params(),
        cost_estimate=pl.CostEstimate(
            flops=8 * tokens * half * width, bytes_accessed=12 * tokens * width, transcendentals=0
        ),
        name="project_last",
    )(chips, attended, acc, gain.reshape(1, width), *halves)


def expert_kernel(count, at, table, *refs):
    blocks, (gate, up, down) = refs[:count], refs[count : count + 3]
    outs = refs[count + 3 : 2 * count + 3]
    tokens, acc = refs[2 * count + 3 :]
    rows = blocks[0].shape[0]
    step = pl.program_id(0)

    @pl.when(step == 0)
    def _():
        for i in range(count):
            tokens[i * rows : (i + 1) * rows, :] = blocks[i][...]

    g = jnp.dot(tokens[...], gate[0], preferred_element_type=F32)
    u = jnp.dot(tokens[...], up[0], preferred_element_type=F32)
    act = (g / (1.0 + jnp.exp(-g)) * u).astype(BF16)
    part = jnp.dot(act, down[0], preferred_element_type=F32)

    @pl.when(step == 0)
    def _():
        acc[...] = part

    @pl.when(step != 0)
    def _():
        acc[...] += part

    @pl.when(step == pl.num_programs(0) - 1)
    def _():
        for i in range(count):
            weight = table[pl.ds(at[i], 1), :]
            weight = jnp.transpose(jnp.broadcast_to(weight, (rows, rows)))
            for j in range(acc.shape[1] // rows):
                cols = slice(j * rows, (j + 1) * rows)
                outs[i][:, cols] = (acc[i * rows : (i + 1) * rows, cols] * weight).astype(BF16)


def expert_blocks(at, table, blocks, gate, up, down):
    count = len(blocks)
    rows, width = blocks[0].shape
    ff = gate.shape[2]
    tile = 256
    return pl.pallas_call(
        functools.partial(expert_kernel, count),
        grid_spec=pltpu.PrefetchScalarGridSpec(
            num_scalar_prefetch=1,
            grid=(ff // tile,),
            in_specs=[whole(*table.shape)]
            + [whole(rows, width)] * count
            + [
                pl.BlockSpec((1, width, tile), lambda f, _: (0, 0, f)),
                pl.BlockSpec((1, width, tile), lambda f, _: (0, 0, f)),
                pl.BlockSpec((1, tile, width), lambda f, _: (0, f, 0)),
            ],
            out_specs=[whole(rows, width)] * count,
            scratch_shapes=[
                pltpu.VMEM((count * rows, width), BF16),
                pltpu.VMEM((count * rows, width), F32),
            ],
        ),
        out_shape=[jax.ShapeDtypeStruct((rows, width), BF16)] * count,
        compiler_params=params(),
        cost_estimate=pl.CostEstimate(
            flops=6 * count * rows * width * ff,
            bytes_accessed=6 * width * ff,
            transcendentals=count * rows * ff,
        ),
        name="experts",
    )(at, table, *blocks, gate, up, down)


class Ring:
    def __init__(self, n):
        self.chips = n // CORES
        self.cycle = [*range(0, self.chips, 2), *range(self.chips - 1, 0, -2)]
        self.far = self.chips // 2

    def step(self, x, by):
        pairs = []
        for p, chip in enumerate(self.cycle):
            to = self.cycle[(p + by) % self.chips]
            pairs += [(chip * CORES + c, to * CORES + c) for c in range(CORES)]
        return lax.ppermute(x, "ctx", pairs)

    def swap(self, x):
        n = self.chips * CORES
        return lax.ppermute(x, "ctx", [(i, i ^ 1) for i in range(n)])

    def table(self, n):
        place = {chip: p for p, chip in enumerate(self.cycle)}
        rows = []
        for i in range(n):
            p = place[i // CORES]
            row = [self.cycle[p]]
            for k in range(1, self.far):
                row += [self.cycle[(p - k) % self.chips], self.cycle[(p + k) % self.chips]]
            rows.append(row + [self.cycle[(p + self.far) % self.chips]])
        return rows

    def gather(self, x):
        half = x.shape[0] // 2
        levels = [[x]]
        up = down = x
        for _ in range(1, self.far):
            up, down = self.step(up, 1), self.step(down, -1)
            levels.append([up, down])
        levels.append([self.step(up[:half], 1), self.step(down[half:], -1)])
        return levels


def xor_gather(x, n):
    x = x[None]
    bit = 1
    while bit < n:
        other = lax.ppermute(x, "ctx", [(i, i ^ bit) for i in range(n)])
        x = jnp.concatenate([x, other], axis=0)
        bit *= 2
    return x


def add(*xs):
    total = xs[0].astype(F32)
    for x in xs[1:]:
        total = total + x.astype(F32)
    return total


def ring_body(
    n,
    queries,
    keys,
    values,
    block_ids,
    out_weight,
    summary_gain,
    norm_gain,
    routes,
    route_scores,
    expert_gate,
    expert_up,
    expert_down,
):
    index = lax.axis_index("ctx")
    core = index % CORES
    ring = Ring(n)
    near = jnp.asarray(ring.table(n), jnp.int32)[index]

    rows_of_weight = ring.gather(out_weight)
    sibling_rows = [[ring.swap(b) for b in level] for level in rows_of_weight]

    small = summarize(block_ids, keys, values, summary_gain, routes, route_scores, n)
    small = xor_gather(small, n)
    attended = attend(jnp.stack([index, index]), queries, keys, values, small[:, : 8 * KVH])
    base = 8 * KVH
    parts = lax.dynamic_index_in_dim(
        small[:, base:].reshape(n, 2, n, HD), index, axis=2, keepdims=False
    ).astype(F32)
    table = parts[:, 0] + parts[:, 1]

    blocks = []
    for mine, theirs in zip(rows_of_weight[:-1], sibling_rows[:-1]):
        for a, b in zip(mine, theirs):
            blocks += [a, b]
    first = jnp.concatenate([core[None], near[:-1]])
    acc = project_first(first, attended, blocks)
    last = jnp.stack([core, near[-1]])
    hidden, projected, normed = project_last(
        last, attended, acc, norm_gain, [*rows_of_weight[-1], *sibling_rows[-1]]
    )

    levels = ring.gather(normed)
    levels[-1] = [jnp.concatenate(levels[-1], axis=0)]
    partial = []
    at = 0
    for level in levels:
        others = [ring.swap(b) for b in level]
        chips = near[at : at + len(level)]
        at += len(level)
        places = jnp.concatenate([chips * CORES + core, chips * CORES + 1 - core]) ^ index
        done = expert_blocks(
            places, table, [*level, *others], expert_gate, expert_up, expert_down
        )
        kept, sent = done[: len(level)], done[len(level) :]
        partial.append([(a, ring.swap(b)) for a, b in zip(kept, sent)])

    half = queries.shape[0] // 2
    [(mine, theirs)] = partial[-1]
    far = add(mine, theirs).astype(BF16)
    up, down = ring.step(far[:half], 1), ring.step(far[half:], -1)
    for k in range(ring.far - 1, 0, -1):
        (behind, behind2), (ahead, ahead2) = partial[k]
        if k == ring.far - 1:
            zero = jnp.zeros_like(up)
            up = jnp.concatenate([up, zero], axis=0)
            down = jnp.concatenate([zero, down], axis=0)
        up = ring.step(add(ahead, ahead2, up).astype(BF16), 1)
        down = ring.step(add(behind, behind2, down).astype(BF16), -1)
    [(mine, theirs)] = partial[0]
    return projected, add(hidden, mine, theirs, up, down).astype(BF16)


def exchange_body(
    n,
    queries,
    keys,
    values,
    block_ids,
    out_weight,
    summary_gain,
    norm_gain,
    routes,
    route_scores,
    expert_gate,
    expert_up,
    expert_down,
):
    tokens_here = queries.shape[0]
    index = lax.axis_index("ctx")
    small = summarize(block_ids, keys, values, summary_gain, routes, route_scores, 0)
    small = lax.all_gather(small, "ctx", axis=0, tiled=False)
    attended = attend(jnp.stack([index, 0 * index]), queries, keys, values, small)
    hidden = jnp.dot(
        attended,
        lax.all_gather(out_weight, "ctx", axis=0, tiled=True),
        preferred_element_type=F32,
    )
    normed = (normalize(hidden) * norm_gain).astype(BF16)
    combine = route_scores / jnp.sum(route_scores, axis=-1, keepdims=True)
    held = expert_gate.shape[0]
    experts_all = held * n
    capacity = capacity_of(tokens_here, experts_all)
    flat_routes = routes.reshape(-1)
    count = tokens_here * TOP
    hits = flat_routes[:, None] == jnp.arange(experts_all, dtype=jnp.int32)[None, :]
    before = jnp.arange(count)[:, None] > jnp.arange(count)[None, :]
    ahead = jnp.dot(before.astype(BF16), hits.astype(BF16), preferred_element_type=F32)
    slot = jnp.sum(jnp.where(hits, ahead, 0.0), axis=-1).astype(jnp.int32)
    target = flat_routes * capacity + slot
    source = jnp.arange(count, dtype=jnp.int32) // TOP
    outgoing = jnp.zeros((experts_all * capacity, D), BF16).at[target].set(normed[source])
    outgoing = outgoing.reshape(experts_all, capacity, D)
    arrived = lax.all_to_all(outgoing, "ctx", split_axis=0, concat_axis=0, tiled=True)
    inputs = (
        arrived.reshape(n, held, capacity, D).transpose(1, 0, 2, 3).reshape(held, n * capacity, D)
    )
    gate = jnp.einsum("erd,edf->erf", inputs, expert_gate, preferred_element_type=F32)
    upper = jnp.einsum("erd,edf->erf", inputs, expert_up, preferred_element_type=F32)
    act = (jax.nn.silu(gate) * upper).astype(BF16)
    result = jnp.einsum("erf,efd->erd", act, expert_down, preferred_element_type=F32)
    result = (
        result.astype(BF16)
        .reshape(held, n, capacity, D)
        .transpose(1, 0, 2, 3)
        .reshape(n * held, capacity, D)
    )
    returned = lax.all_to_all(result, "ctx", split_axis=0, concat_axis=0, tiled=True)
    returned = returned.reshape(experts_all * capacity, D)
    picked = jnp.take(returned, target, axis=0).reshape(tokens_here, TOP, D)
    blended = jnp.sum(combine[:, :, None] * picked.astype(F32), axis=1)
    return (hidden.astype(BF16), (hidden + blended).astype(BF16))


def capacity_of(tokens, experts):
    return max(2, 5 * tokens * TOP // (4 * experts))


def solution(mesh):
    n = mesh.shape["ctx"]

    def body(*args):
        tokens, held = args[0].shape[0], args[9].shape[0]
        dense = tokens <= 2 * capacity_of(tokens, held * n) and held == 1
        fits = n % 4 == 0 and n & (n - 1) == 0
        return (ring_body if dense and fits else exchange_body)(n, *args)

    in_specs = (
        P(("groups", "ctx"), None),
        P(("groups", "ctx"), None),
        P(("groups", "ctx"), None),
        P(("groups", "ctx")),
        P("ctx", None),
        P(),
        P(),
        P(("groups", "ctx"), None),
        P(("groups", "ctx"), None),
        P("ctx", None, None),
        P("ctx", None, None),
        P("ctx", None, None),
    )
    out_specs = (P(("groups", "ctx"), None), P(("groups", "ctx"), None))
    return jax.shard_map(body, mesh=mesh, in_specs=in_specs, out_specs=out_specs, check_vma=False)
```

```python
import functools
import math

import jax
import jax.numpy as jnp
from jax import lax
from jax.experimental import pallas as pl
from jax.experimental.pallas import tpu as pltpu
from jax.sharding import PartitionSpec as P

D = 2048
HQ = 16
KVH = 4
HD = 128
TOP = 8
NB = 4
CORES = 2
VMEM_BYTES = 48 * 1024 * 1024
F32 = jnp.float32
BF16 = jnp.bfloat16


def normalize(x):
    return x * lax.rsqrt(jnp.mean(x * x, axis=-1, keepdims=True) + 1e-06)


def params():
    return pltpu.CompilerParams(vmem_limit_bytes=VMEM_BYTES)


def whole(*shape):
    return pl.BlockSpec(shape, lambda *_: (0,) * len(shape))


def summary_kernel(experts, ids, keys, values, gain, routes, scores, out, rows):
    tokens = ids.shape[1]
    block = lax.broadcasted_iota(jnp.int32, (8, tokens), 0)
    member = (ids[...] == block) & (block < NB)
    ones = jnp.where(member, 1.0, 0.0).astype(F32)
    count = jnp.maximum(jnp.sum(ones, axis=-1, keepdims=True), 1.0)
    indicator = ones.astype(BF16)
    kmean = jnp.dot(indicator, keys[...], preferred_element_type=F32) / count
    vmean = jnp.dot(indicator, values[...], preferred_element_type=F32) / count
    for g in range(KVH):
        cols = slice(g * HD, (g + 1) * HD)
        rows[8 * g : 8 * g + NB, :] = (normalize(kmean[:, cols]) * gain[...])[:NB]
        rows[8 * g + NB : 8 * g + 2 * NB, :] = normalize(vmean[:, cols])[:NB]
    base = 8 * KVH
    if experts:
        combine = scores[...] / jnp.sum(scores[...], axis=0, keepdims=True)
        expert = lax.broadcasted_iota(jnp.int32, (experts, tokens), 0)
        table = jnp.zeros((experts, tokens), F32)
        for k in range(TOP):
            table += jnp.where(routes[k : k + 1, :] == expert, combine[k : k + 1, :], 0.0)
        high = table.astype(BF16).astype(F32)
        rows[base : base + experts, :] = high
        rows[base + experts : base + 2 * experts, :] = table - high
    out[...] = rows[...].astype(BF16)


def summarize(ids, keys, values, gain, routes, scores, experts):
    tokens = ids.shape[0]
    height = 8 * KVH + 2 * experts
    return pl.pallas_call(
        functools.partial(summary_kernel, experts),
        out_shape=jax.ShapeDtypeStruct((height, HD), BF16),
        scratch_shapes=[pltpu.VMEM((height, HD), F32)],
        compiler_params=params(),
        name="summaries",
    )(ids.reshape(1, tokens), keys, values, gain.reshape(1, HD), routes.T, scores.T)


def attention_kernel(me, queries, keys, values, gathered, attended):
    tokens = queries.shape[0]
    group = HQ // KVH
    scale = 1.0 / math.sqrt(HD)
    shards = gathered.shape[0]
    wide = shards * 2 * NB
    row = lax.broadcasted_iota(jnp.int32, (tokens, tokens), 0)
    col = lax.broadcasted_iota(jnp.int32, (tokens, tokens), 1)
    causal = row >= col
    place = lax.broadcasted_iota(jnp.int32, (tokens, wide), 1)
    owner = (place // (2 * NB)) ^ me[1]
    earlier = (owner < me[0]) & (place % (2 * NB) < NB)
    seen = jnp.concatenate([causal, earlier], axis=1)
    for g in range(KVH):
        cols = slice(g * HD, (g + 1) * HD)
        pairs = gathered[:, 16 * (g // 2) : 16 * (g // 2) + 16, :].astype(F32)
        half = 8 * (g % 2)
        remote = pairs[:, half : half + 8, :].reshape(wide, HD)
        key_all = jnp.concatenate([keys[:, cols], remote.astype(BF16)], axis=0)
        shifted = pltpu.roll(remote, wide - NB, 0)
        value_all = jnp.concatenate([values[:, cols], shifted.astype(BF16)], axis=0)
        for i in range(group):
            h = g * group + i
            head = slice(h * HD, (h + 1) * HD)
            scores = (
                lax.dot_general(
                    queries[:, head],
                    key_all,
                    (((1,), (1,)), ((), ())),
                    preferred_element_type=F32,
                )
                * scale
            )
            scores = jnp.where(seen, scores, -jnp.inf)
            top = jnp.max(scores, axis=-1, keepdims=True)
            expo = jnp.exp(scores - top)
            weights = (expo / jnp.sum(expo, axis=-1, keepdims=True)).astype(BF16)
            attended[:, head] = jnp.dot(
                weights, value_all, preferred_element_type=F32
            ).astype(BF16)


def attend(me, queries, keys, values, gathered):
    tokens = queries.shape[0]
    return pl.pallas_call(
        attention_kernel,
        grid_spec=pltpu.PrefetchScalarGridSpec(
            num_scalar_prefetch=1,
            grid=(1,),
            in_specs=[whole(*a.shape) for a in (queries, keys, values, gathered)],
            out_specs=whole(tokens, HQ * HD),
        ),
        out_shape=jax.ShapeDtypeStruct((tokens, HQ * HD), BF16),
        compiler_params=params(),
        cost_estimate=pl.CostEstimate(
            flops=4 * HQ * HD * tokens * 2 * tokens,
            bytes_accessed=2 * 4 * tokens * HQ * HD,
            transcendentals=HQ * tokens * 2 * tokens,
        ),
        name="attention",
    )(me, queries, keys, values, gathered)


def project_first_kernel(chips, attended, *refs):
    blocks, acc, pair = refs[:-2], refs[-2], refs[-1]
    rows = blocks[0].shape[0]
    mine = chips[0]
    total = None
    for i in range(len(blocks) // 2):
        pair[pl.ds(pl.multiple_of(mine * rows, rows), rows), :] = blocks[2 * i][...]
        pair[pl.ds(pl.multiple_of((1 - mine) * rows, rows), rows), :] = blocks[2 * i + 1][...]
        at = pl.multiple_of(chips[i + 1] * 2 * rows, 2 * rows)
        part = jnp.dot(
            attended[:, pl.ds(at, 2 * rows)], pair[...], preferred_element_type=F32
        )
        if i == 0:
            acc[...] = part
        else:
            acc[...] += part


def project_first(chips, attended, blocks):
    tokens = attended.shape[0]
    rows, width = blocks[0].shape
    return pl.pallas_call(
        project_first_kernel,
        grid_spec=pltpu.PrefetchScalarGridSpec(
            num_scalar_prefetch=1,
            grid=(1,),
            in_specs=[whole(*attended.shape)] + [whole(rows, width)] * len(blocks),
            out_specs=whole(tokens, width),
            scratch_shapes=[pltpu.VMEM((2 * rows, width), BF16)],
        ),
        out_shape=jax.ShapeDtypeStruct((tokens, width), F32),
        compiler_params=params(),
        cost_estimate=pl.CostEstimate(
            flops=2 * tokens * rows * width * len(blocks),
            bytes_accessed=2 * rows * width * len(blocks),
            transcendentals=0,
        ),
        name="project_first",
    )(chips, attended, *blocks)


def project_last_kernel(chips, attended, acc, gain, a, b, c, d, hidden, projected, normed, pair):
    half = a.shape[0]
    rows = 2 * half
    mine = chips[0]
    own = pl.multiple_of(mine * rows, rows)
    other = pl.multiple_of((1 - mine) * rows, rows)
    pair[pl.ds(own, half), :] = a[...]
    pair[pl.ds(own + half, half), :] = b[...]
    pair[pl.ds(other, half), :] = c[...]
    pair[pl.ds(other + half, half), :] = d[...]
    at = pl.multiple_of(chips[1] * 2 * rows, 2 * rows)
    total = acc[...] + jnp.dot(
        attended[:, pl.ds(at, 2 * rows)], pair[...], preferred_element_type=F32
    )
    hidden[...] = total
    projected[...] = total.astype(BF16)
    normed[...] = (normalize(total) * gain[...]).astype(BF16)


def project_last(chips, attended, acc, gain, halves):
    tokens, width = acc.shape
    half = halves[0].shape[0]
    return pl.pallas_call(
        project_last_kernel,
        grid_spec=pltpu.PrefetchScalarGridSpec(
            num_scalar_prefetch=1,
            grid=(1,),
            in_specs=[whole(*attended.shape), whole(tokens, width), whole(1, width)]
            + [whole(half, width)] * 4,
            out_specs=[whole(tokens, width)] * 3,
            scratch_shapes=[pltpu.VMEM((4 * half, width), BF16)],
        ),
        out_shape=[
            jax.ShapeDtypeStruct((tokens, width), F32),
            jax.ShapeDtypeStruct((tokens, width), BF16),
            jax.ShapeDtypeStruct((tokens, width), BF16),
        ],
        compiler_params=params(),
        cost_estimate=pl.CostEstimate(
            flops=8 * tokens * half * width, bytes_accessed=12 * tokens * width, transcendentals=0
        ),
        name="project_last",
    )(chips, attended, acc, gain.reshape(1, width), *halves)


def expert_kernel(count, at, table, *refs):
    blocks, (gate, up, down) = refs[:count], refs[count : count + 3]
    outs = refs[count + 3 : 2 * count + 3]
    tokens, acc = refs[2 * count + 3 :]
    rows = blocks[0].shape[0]
    step = pl.program_id(0)

    @pl.when(step == 0)
    def _():
        for i in range(count):
            tokens[i * rows : (i + 1) * rows, :] = blocks[i][...]

    g = jnp.dot(tokens[...], gate[0], preferred_element_type=F32)
    u = jnp.dot(tokens[...], up[0], preferred_element_type=F32)
    act = (g / (1.0 + jnp.exp(-g)) * u).astype(BF16)
    part = jnp.dot(act, down[0], preferred_element_type=F32)

    @pl.when(step == 0)
    def _():
        acc[...] = part

    @pl.when(step != 0)
    def _():
        acc[...] += part

    @pl.when(step == pl.num_programs(0) - 1)
    def _():
        for i in range(count):
            weight = table[pl.ds(at[i], 1), :]
            weight = jnp.transpose(jnp.broadcast_to(weight, (rows, rows)))
            for j in range(acc.shape[1] // rows):
                cols = slice(j * rows, (j + 1) * rows)
                outs[i][:, cols] = (acc[i * rows : (i + 1) * rows, cols] * weight).astype(BF16)


def expert_blocks(at, table, blocks, gate, up, down):
    count = len(blocks)
    rows, width = blocks[0].shape
    ff = gate.shape[2]
    tile = 256
    return pl.pallas_call(
        functools.partial(expert_kernel, count),
        grid_spec=pltpu.PrefetchScalarGridSpec(
            num_scalar_prefetch=1,
            grid=(ff // tile,),
            in_specs=[whole(*table.shape)]
            + [whole(rows, width)] * count
            + [
                pl.BlockSpec((1, width, tile), lambda f, _: (0, 0, f)),
                pl.BlockSpec((1, width, tile), lambda f, _: (0, 0, f)),
                pl.BlockSpec((1, tile, width), lambda f, _: (0, f, 0)),
            ],
            out_specs=[whole(rows, width)] * count,
            scratch_shapes=[
                pltpu.VMEM((count * rows, width), BF16),
                pltpu.VMEM((count * rows, width), F32),
            ],
        ),
        out_shape=[jax.ShapeDtypeStruct((rows, width), BF16)] * count,
        compiler_params=params(),
        cost_estimate=pl.CostEstimate(
            flops=6 * count * rows * width * ff,
            bytes_accessed=6 * width * ff,
            transcendentals=count * rows * ff,
        ),
        name="experts",
    )(at, table, *blocks, gate, up, down)


class Ring:
    def __init__(self, n):
        self.chips = n // CORES
        self.cycle = [*range(0, self.chips, 2), *range(self.chips - 1, 0, -2)]
        self.far = self.chips // 2

    def step(self, x, by):
        pairs = []
        for p, chip in enumerate(self.cycle):
            to = self.cycle[(p + by) % self.chips]
            pairs += [(chip * CORES + c, to * CORES + c) for c in range(CORES)]
        return lax.ppermute(x, "ctx", pairs)

    def swap(self, x):
        n = self.chips * CORES
        return lax.ppermute(x, "ctx", [(i, i ^ 1) for i in range(n)])

    def table(self, n):
        place = {chip: p for p, chip in enumerate(self.cycle)}
        rows = []
        for i in range(n):
            p = place[i // CORES]
            row = [self.cycle[p]]
            for k in range(1, self.far):
                row += [self.cycle[(p - k) % self.chips], self.cycle[(p + k) % self.chips]]
            rows.append(row + [self.cycle[(p + self.far) % self.chips]])
        return rows


def xor_step(x, bit, n):
    other = lax.ppermute(x, "ctx", [(i, i ^ bit) for i in range(n)])
    return jnp.concatenate([x, other], axis=0)


def xor_rest(x, n):
    while x.shape[0] < n:
        x = xor_step(x, x.shape[0], n)
    return x


def after(x, *earlier):
    return lax.optimization_barrier((x, earlier))[0]


def add(*xs):
    total = xs[0].astype(F32)
    for x in xs[1:]:
        total = total + x.astype(F32)
    return total


def ring_body(
    n,
    queries,
    keys,
    values,
    block_ids,
    out_weight,
    summary_gain,
    norm_gain,
    routes,
    route_scores,
    expert_gate,
    expert_up,
    expert_down,
):
    index = lax.axis_index("ctx")
    core = index % CORES
    ring = Ring(n)
    near = jnp.asarray(ring.table(n), jnp.int32)[index]

    half = queries.shape[0] // 2
    small = summarize(block_ids, keys, values, summary_gain, routes, route_scores, n)
    small = xor_step(xor_step(small[None], 1, n), 2, n)
    up, down = ring.step(out_weight, 1), ring.step(out_weight, -1)
    blocks = [out_weight, ring.swap(out_weight)]
    for k in range(1, ring.far):
        if k == 1:
            up, down = after(up, small), after(down, small)
            small = xor_rest(small, n)
            attended = attend(jnp.stack([index, index]), queries, keys, values, small[:, : 8 * KVH])
        if k == 2:
            up, down = after(up, attended), after(down, attended)
        blocks += [up, ring.swap(up), down, ring.swap(down)]
        if k < ring.far - 1:
            up, down = ring.step(up, 1), ring.step(down, -1)
    up, down = ring.step(up[:half], 1), ring.step(down[half:], -1)
    base = 8 * KVH
    parts = lax.dynamic_index_in_dim(
        small[:, base:].reshape(n, 2, n, HD), index, axis=2, keepdims=False
    ).astype(F32)
    table = parts[:, 0] + parts[:, 1]
    first = jnp.concatenate([core[None], near[:-1]])
    acc = project_first(first, attended, blocks)
    up, down = after(up, acc), after(down, acc)
    last = jnp.stack([core, near[-1]])
    hidden, projected, normed = project_last(
        last, attended, acc, norm_gain, [up, down, ring.swap(up), ring.swap(down)]
    )

    at = 0
    partial = []

    def experts(level):
        nonlocal at
        others = [ring.swap(b) for b in level]
        chips = near[at : at + len(level)]
        at += len(level)
        places = jnp.concatenate([chips * CORES + core, chips * CORES + 1 - core]) ^ index
        done = expert_blocks(
            places, table, [*level, *others], expert_gate, expert_up, expert_down
        )
        kept, sent = done[: len(level)], done[len(level) :]
        partial.append([(a, ring.swap(b)) for a, b in zip(kept, sent)])
        return kept[0]

    level = [normed]
    up, down = ring.step(normed, 1), ring.step(normed, -1)
    for k in range(1, ring.far):
        done = experts(level)
        up, down = after(up, done), after(down, done)
        level = [up, down]
        if k < ring.far - 1:
            up, down = ring.step(up, 1), ring.step(down, -1)
    up, down = ring.step(up[:half], 1), ring.step(down[half:], -1)
    late = level
    at += 2
    experts([jnp.concatenate([up, down], axis=0)])
    far = partial.pop()
    at -= 3
    experts([after(b, far[0][0]) for b in late])
    partial.append(far)

    [(mine, theirs)] = partial[-1]
    far = add(mine, theirs).astype(BF16)
    up, down = ring.step(far[:half], 1), ring.step(far[half:], -1)
    for k in range(ring.far - 1, 0, -1):
        (behind, behind2), (ahead, ahead2) = partial[k]
        if k == ring.far - 1:
            zero = jnp.zeros_like(up)
            up = jnp.concatenate([up, zero], axis=0)
            down = jnp.concatenate([zero, down], axis=0)
        up = ring.step(add(ahead, ahead2, up).astype(BF16), 1)
        down = ring.step(add(behind, behind2, down).astype(BF16), -1)
    [(mine, theirs)] = partial[0]
    return projected, add(hidden, mine, theirs, up, down).astype(BF16)


def exchange_body(
    n,
    queries,
    keys,
    values,
    block_ids,
    out_weight,
    summary_gain,
    norm_gain,
    routes,
    route_scores,
    expert_gate,
    expert_up,
    expert_down,
):
    tokens_here = queries.shape[0]
    index = lax.axis_index("ctx")
    small = summarize(block_ids, keys, values, summary_gain, routes, route_scores, 0)
    small = lax.all_gather(small, "ctx", axis=0, tiled=False)
    attended = attend(jnp.stack([index, 0 * index]), queries, keys, values, small)
    hidden = jnp.dot(
        attended,
        lax.all_gather(out_weight, "ctx", axis=0, tiled=True),
        preferred_element_type=F32,
    )
    normed = (normalize(hidden) * norm_gain).astype(BF16)
    combine = route_scores / jnp.sum(route_scores, axis=-1, keepdims=True)
    held = expert_gate.shape[0]
    experts_all = held * n
    capacity = capacity_of(tokens_here, experts_all)
    flat_routes = routes.reshape(-1)
    count = tokens_here * TOP
    hits = flat_routes[:, None] == jnp.arange(experts_all, dtype=jnp.int32)[None, :]
    before = jnp.arange(count)[:, None] > jnp.arange(count)[None, :]
    ahead = jnp.dot(before.astype(BF16), hits.astype(BF16), preferred_element_type=F32)
    slot = jnp.sum(jnp.where(hits, ahead, 0.0), axis=-1).astype(jnp.int32)
    target = flat_routes * capacity + slot
    source = jnp.arange(count, dtype=jnp.int32) // TOP
    outgoing = jnp.zeros((experts_all * capacity, D), BF16).at[target].set(normed[source])
    outgoing = outgoing.reshape(experts_all, capacity, D)
    arrived = lax.all_to_all(outgoing, "ctx", split_axis=0, concat_axis=0, tiled=True)
    inputs = (
        arrived.reshape(n, held, capacity, D).transpose(1, 0, 2, 3).reshape(held, n * capacity, D)
    )
    gate = jnp.einsum("erd,edf->erf", inputs, expert_gate, preferred_element_type=F32)
    upper = jnp.einsum("erd,edf->erf", inputs, expert_up, preferred_element_type=F32)
    act = (jax.nn.silu(gate) * upper).astype(BF16)
    result = jnp.einsum("erf,efd->erd", act, expert_down, preferred_element_type=F32)
    result = (
        result.astype(BF16)
        .reshape(held, n, capacity, D)
        .transpose(1, 0, 2, 3)
        .reshape(n * held, capacity, D)
    )
    returned = lax.all_to_all(result, "ctx", split_axis=0, concat_axis=0, tiled=True)
    returned = returned.reshape(experts_all * capacity, D)
    picked = jnp.take(returned, target, axis=0).reshape(tokens_here, TOP, D)
    blended = jnp.sum(combine[:, :, None] * picked.astype(F32), axis=1)
    return (hidden.astype(BF16), (hidden + blended).astype(BF16))


def capacity_of(tokens, experts):
    return max(2, 5 * tokens * TOP // (4 * experts))


def solution(mesh):
    n = mesh.shape["ctx"]

    def body(*args):
        tokens, held = args[0].shape[0], args[9].shape[0]
        dense = tokens <= 2 * capacity_of(tokens, held * n) and held == 1
        fits = n % 4 == 0 and n & (n - 1) == 0
        return (ring_body if dense and fits else exchange_body)(n, *args)

    in_specs = (
        P(("groups", "ctx"), None),
        P(("groups", "ctx"), None),
        P(("groups", "ctx"), None),
        P(("groups", "ctx")),
        P("ctx", None),
        P(),
        P(),
        P(("groups", "ctx"), None),
        P(("groups", "ctx"), None),
        P("ctx", None, None),
        P("ctx", None, None),
        P("ctx", None, None),
    )
    out_specs = (P(("groups", "ctx"), None), P(("groups", "ctx"), None))
    return jax.shard_map(body, mesh=mesh, in_specs=in_specs, out_specs=out_specs, check_vma=False)
```

```python
import functools
import math

import jax
import jax.numpy as jnp
from jax import lax
from jax.experimental import pallas as pl
from jax.experimental.pallas import tpu as pltpu
from jax.sharding import PartitionSpec as P

D = 2048
HQ = 16
KVH = 4
HD = 128
TOP = 8
NB = 4
CORES = 2
VMEM_BYTES = 16 * 1024 * 1024
F32 = jnp.float32
BF16 = jnp.bfloat16


def normalize(x):
    return x * lax.rsqrt(jnp.mean(x * x, axis=-1, keepdims=True) + 1e-06)


def params():
    return pltpu.CompilerParams(vmem_limit_bytes=VMEM_BYTES)


def whole(*shape):
    return pl.BlockSpec(shape, lambda *_: (0,) * len(shape))


def summary_kernel(experts, ids, keys, values, gain, routes, scores, out, rows):
    tokens = ids.shape[1]
    block = lax.broadcasted_iota(jnp.int32, (8, tokens), 0)
    member = (ids[...] == block) & (block < NB)
    ones = jnp.where(member, 1.0, 0.0).astype(F32)
    count = jnp.maximum(jnp.sum(ones, axis=-1, keepdims=True), 1.0)
    indicator = ones.astype(BF16)
    kmean = jnp.dot(indicator, keys[...], preferred_element_type=F32) / count
    vmean = jnp.dot(indicator, values[...], preferred_element_type=F32) / count
    for g in range(KVH):
        cols = slice(g * HD, (g + 1) * HD)
        rows[8 * g : 8 * g + NB, :] = (normalize(kmean[:, cols]) * gain[...])[:NB]
        rows[8 * g + NB : 8 * g + 2 * NB, :] = normalize(vmean[:, cols])[:NB]
    base = 8 * KVH
    if experts:
        combine = scores[...] / jnp.sum(scores[...], axis=0, keepdims=True)
        expert = lax.broadcasted_iota(jnp.int32, (experts, tokens), 0)
        table = jnp.zeros((experts, tokens), F32)
        for k in range(TOP):
            table += jnp.where(routes[k : k + 1, :] == expert, combine[k : k + 1, :], 0.0)
        high = table.astype(BF16).astype(F32)
        rows[base : base + experts, :] = high
        rows[base + experts : base + 2 * experts, :] = table - high
    out[...] = rows[...].astype(BF16)


def summarize(ids, keys, values, gain, routes, scores, experts):
    tokens = ids.shape[0]
    height = 8 * KVH + 2 * experts
    return pl.pallas_call(
        functools.partial(summary_kernel, experts),
        out_shape=jax.ShapeDtypeStruct((height, HD), BF16),
        scratch_shapes=[pltpu.VMEM((height, HD), F32)],
        compiler_params=params(),
        name="summaries",
    )(ids.reshape(1, tokens), keys, values, gain.reshape(1, HD), routes.T, scores.T)


def attention_kernel(me, queries, keys, values, gathered, attended):
    tokens = queries.shape[0]
    group = HQ // KVH
    scale = 1.0 / math.sqrt(HD)
    shards = gathered.shape[0]
    wide = shards * 2 * NB
    row = lax.broadcasted_iota(jnp.int32, (tokens, tokens), 0)
    col = lax.broadcasted_iota(jnp.int32, (tokens, tokens), 1)
    causal = row >= col
    place = lax.broadcasted_iota(jnp.int32, (tokens, wide), 1)
    owner = (place // (2 * NB)) ^ me[1]
    earlier = (owner < me[0]) & (place % (2 * NB) < NB)
    seen = jnp.concatenate([causal, earlier], axis=1)
    for g in range(KVH):
        cols = slice(g * HD, (g + 1) * HD)
        pairs = gathered[:, 16 * (g // 2) : 16 * (g // 2) + 16, :].astype(F32)
        half = 8 * (g % 2)
        remote = pairs[:, half : half + 8, :].reshape(wide, HD)
        key_all = jnp.concatenate([keys[:, cols], remote.astype(BF16)], axis=0)
        shifted = pltpu.roll(remote, wide - NB, 0)
        value_all = jnp.concatenate([values[:, cols], shifted.astype(BF16)], axis=0)
        for i in range(group):
            h = g * group + i
            head = slice(h * HD, (h + 1) * HD)
            scores = (
                lax.dot_general(
                    queries[:, head],
                    key_all,
                    (((1,), (1,)), ((), ())),
                    preferred_element_type=F32,
                )
                * scale
            )
            scores = jnp.where(seen, scores, -jnp.inf)
            top = jnp.max(scores, axis=-1, keepdims=True)
            expo = jnp.exp(scores - top)
            weights = (expo / jnp.sum(expo, axis=-1, keepdims=True)).astype(BF16)
            attended[:, head] = jnp.dot(
                weights, value_all, preferred_element_type=F32
            ).astype(BF16)


def attend(me, queries, keys, values, gathered):
    tokens = queries.shape[0]
    return pl.pallas_call(
        attention_kernel,
        grid_spec=pltpu.PrefetchScalarGridSpec(
            num_scalar_prefetch=1,
            grid=(1,),
            in_specs=[whole(*a.shape) for a in (queries, keys, values, gathered)],
            out_specs=whole(tokens, HQ * HD),
        ),
        out_shape=jax.ShapeDtypeStruct((tokens, HQ * HD), BF16),
        compiler_params=params(),
        cost_estimate=pl.CostEstimate(
            flops=4 * HQ * HD * tokens * 2 * tokens,
            bytes_accessed=2 * 4 * tokens * HQ * HD,
            transcendentals=HQ * tokens * 2 * tokens,
        ),
        name="attention",
    )(me, queries, keys, values, gathered)


def smem():
    return pl.BlockSpec(memory_space=pltpu.SMEM)


def vmem():
    return pl.BlockSpec(memory_space=pltpu.VMEM)


def pair_up(here, pair, own, other):
    rows = pair.shape[0] // CORES
    at = pl.multiple_of(here[0] * rows, rows)
    for i, block in enumerate(own):
        step = i * block.shape[0]
        pair[pl.ds(at + step, block.shape[0]), :] = block[...]
    at = pl.multiple_of((1 - here[0]) * rows, rows)
    for i, block in enumerate(other):
        step = i * block.shape[0]
        pair[pl.ds(at + step, block.shape[0]), :] = block[...]


def project_first_kernel(levels, here, tokens, *refs):
    blocks, acc, pair = refs[:-2], refs[-2], refs[-1]
    rows = pair.shape[1]
    for i in range(levels):
        pair_up(here, pair.at[i], [blocks[2 * i]], [blocks[2 * i + 1]])
    for i in range(levels):
        at = pl.multiple_of(here[1 + i] * rows, rows)
        part = jnp.dot(tokens[:, pl.ds(at, rows)], pair[i], preferred_element_type=F32)
        if i == 0:
            acc[...] = part
        else:
            acc[...] += part


def project_first(here, tokens, blocks):
    rows, width = blocks[0].shape
    levels = len(blocks) // 2
    return pl.pallas_call(
        functools.partial(project_first_kernel, levels),
        in_specs=[smem()] + [vmem()] * (1 + len(blocks)),
        out_specs=vmem(),
        out_shape=jax.ShapeDtypeStruct((tokens.shape[0], width), F32),
        scratch_shapes=[pltpu.VMEM((levels, 2 * rows, width), BF16)],
        compiler_params=params(),
        cost_estimate=pl.CostEstimate(
            flops=2 * tokens.shape[0] * rows * width * len(blocks),
            bytes_accessed=2 * rows * width * len(blocks),
            transcendentals=0,
        ),
        name="project_first",
    )(here, tokens, *blocks)


def project_last_kernel(at, here, tokens, acc, gain, a, b, c, d, hidden, projected, normed, pair):
    rows = pair.shape[0]
    pair_up(here, pair, [a, b], [c, d])
    columns = pl.ds(pl.multiple_of(here[at] * rows, rows), rows)
    total = acc[...] + jnp.dot(tokens[:, columns], pair[...], preferred_element_type=F32)
    hidden[...] = total
    projected[...] = total.astype(BF16)
    normed[...] = (normalize(total) * gain[...]).astype(BF16)


def project_last(at, here, tokens, acc, gain, halves):
    count, width = acc.shape
    half = halves[0].shape[0]
    return pl.pallas_call(
        functools.partial(project_last_kernel, at),
        in_specs=[smem()] + [vmem()] * 7,
        out_specs=[vmem()] * 3,
        out_shape=[
            jax.ShapeDtypeStruct((count, width), F32),
            jax.ShapeDtypeStruct((count, width), BF16),
            jax.ShapeDtypeStruct((count, width), BF16),
        ],
        scratch_shapes=[pltpu.VMEM((4 * half, width), BF16)],
        compiler_params=params(),
        cost_estimate=pl.CostEstimate(
            flops=8 * count * half * width, bytes_accessed=12 * count * width, transcendentals=0
        ),
        name="project_last",
    )(here, tokens, acc, gain.reshape(1, width), *halves)


def expert_kernel(places, here, table, *refs):
    count = len(places)
    own = count // 2
    blocks, (gate, up, down) = refs[:count], refs[count : count + 3]
    outs = refs[count + 3 : count + 3 + own]
    sent = refs[count + 3 + own]
    tokens, act, scale = refs[count + 4 + own :]
    rows, depth = blocks[0].shape
    lanes = table.shape[1]
    ff = gate.shape[2]
    tile = 256
    for i in range(count):
        tokens[i * rows : (i + 1) * rows, :] = blocks[i][...]
        weight = table[pl.ds(here[places[i]], 1), :]
        weight = jnp.transpose(jnp.broadcast_to(weight, (lanes, lanes)))
        scale[i * rows : (i + 1) * rows, :] = weight
    for f in range(0, ff, tile):
        cols = slice(f, f + tile)
        g = jnp.dot(tokens[...], gate[0, :, cols], preferred_element_type=F32)
        u = jnp.dot(tokens[...], up[0, :, cols], preferred_element_type=F32)
        act[:, cols] = (g / (1.0 + jnp.exp(-g)) * u).astype(BF16)
    for d in range(0, depth, tile):
        cols = slice(d, d + tile)
        part = jnp.dot(act[...], down[0, :, cols], preferred_element_type=F32)
        weight = jnp.concatenate([scale[...]] * (tile // lanes), axis=1)
        part = (part * weight).astype(BF16)
        for i in range(own):
            outs[i][:, cols] = part[i * rows : (i + 1) * rows]
        sent[:, cols] = part[own * rows :]


def expert_blocks(places, here, table, blocks, gate, up, down):
    count = len(blocks)
    own = count // 2
    rows, width = blocks[0].shape
    ff = gate.shape[2]
    return pl.pallas_call(
        functools.partial(expert_kernel, places),
        in_specs=[smem()] + [vmem()] * (1 + count + 3),
        out_specs=[vmem()] * (own + 1),
        out_shape=[jax.ShapeDtypeStruct((rows, width), BF16)] * own
        + [jax.ShapeDtypeStruct((own * rows, width), BF16)],
        scratch_shapes=[
            pltpu.VMEM((count * rows, width), BF16),
            pltpu.VMEM((count * rows, ff), BF16),
            pltpu.VMEM((count * rows, table.shape[1]), F32),
        ],
        compiler_params=params(),
        cost_estimate=pl.CostEstimate(flops=0, bytes_accessed=0, transcendentals=0),
        name="experts",
    )(here, table, *blocks, gate, up, down)


class Ring:
    def __init__(self, n):
        self.chips = n // CORES
        self.cycle = [*range(0, self.chips, 2), *range(self.chips - 1, 0, -2)]
        self.far = self.chips // 2

    def step(self, x, by, label):
        pairs = []
        for p, chip in enumerate(self.cycle):
            to = self.cycle[(p + by) % self.chips]
            pairs += [(chip * CORES + c, to * CORES + c) for c in range(CORES)]
        with jax.named_scope(label + ("_up" if by > 0 else "_down")):
            return lax.ppermute(x, "ctx", pairs)

    def swap(self, x):
        n = self.chips * CORES
        with jax.named_scope("swap_cores"):
            return lax.ppermute(x, "ctx", [(i, i ^ 1) for i in range(n)])

    def table(self, n):
        place = {chip: p for p, chip in enumerate(self.cycle)}
        rows = []
        for i in range(n):
            p, core = place[i // CORES], i % CORES
            chips = [self.cycle[p]]
            for k in range(1, self.far):
                chips += [self.cycle[(p - k) % self.chips], self.cycle[(p + k) % self.chips]]
            chips.append(self.cycle[(p + self.far) % self.chips])
            own = [(chip * CORES + core) ^ i for chip in chips]
            other = [(chip * CORES + 1 - core) ^ i for chip in chips]
            rows.append([core, *chips, *own, *other])
        return rows


def xor_round(x, count, n):
    m = x.shape[0]
    with jax.named_scope("summary_round"):
        others = [
            lax.ppermute(x, "ctx", [(i, i ^ (m * c)) for i in range(n)]) for c in range(1, count)
        ]
    return jnp.concatenate([x, *others], axis=0)


def after(x, *earlier):
    return lax.optimization_barrier((x, earlier))[0]


def add(*xs):
    total = xs[0].astype(F32)
    for x in xs[1:]:
        total = total + x.astype(F32)
    return total.astype(BF16)


def ring_body(
    n,
    queries,
    keys,
    values,
    block_ids,
    out_weight,
    summary_gain,
    norm_gain,
    routes,
    route_scores,
    expert_gate,
    expert_up,
    expert_down,
):
    index = lax.axis_index("ctx")
    core = index % CORES
    ring = Ring(n)
    here = jnp.asarray(ring.table(n), jnp.int32)[index]
    half = queries.shape[0] // 2

    def both(pair, *earlier):
        return [after(x, *earlier) for x in pair]

    def forward(pair, label):
        return [ring.step(pair[0], 1, label), ring.step(pair[1], -1, label)]

    def forward_far(pair, label):
        return forward([pair[0][:half], pair[1][half:]], label)

    pair = forward([out_weight, out_weight], "weight_1")
    blocks = [out_weight, ring.swap(out_weight)]
    small = summarize(block_ids, keys, values, summary_gain, routes, route_scores, n)[None]
    small = xor_round(xor_round(small, 2, n), 4, n)
    for k in range(1, ring.far):
        if k == 1:
            small = after(small, *pair)
            while small.shape[0] < n:
                small = xor_round(small, 2, n)
        if k == 2:
            pair = both(pair, small)
            attended = attend(jnp.stack([index, index]), queries, keys, values, small[:, : 8 * KVH])
        if k == 3:
            pair = both(pair, attended)
        for x in pair:
            blocks += [x, ring.swap(x)]
        if k < ring.far - 1:
            pair = forward(pair, "weight_" + str(k + 1))
    pair = forward_far(pair, "weight_far")
    base = 8 * KVH
    parts = lax.dynamic_index_in_dim(
        small[:, base:].reshape(n, 2, n, HD), index, axis=2, keepdims=False
    ).astype(F32)
    table = parts[:, 0] + parts[:, 1]
    acc = project_first(here, attended, blocks)
    pair = both(pair, acc, table)
    hidden, projected, normed = project_last(
        ring.chips, here, attended, acc, norm_gain, [*pair, *(ring.swap(x) for x in pair)]
    )

    def experts(level, chips):
        others = [ring.swap(x) for x in level]
        places = [1 + ring.chips + c for c in chips] + [1 + 2 * ring.chips + c for c in chips]
        *kept, sent = expert_blocks(
            tuple(places), here, table, [*level, *others], expert_gate, expert_up, expert_down
        )
        return [*kept, ring.swap(sent)]

    pair = forward([normed, normed], "token_1")
    results = [experts([normed], [0])]
    for k in range(1, ring.far):
        pair = both(pair, results[-1][0])
        level = pair
        if k < ring.far - 1:
            pair = forward(pair, "token_" + str(k + 1))
        else:
            pair = forward_far(pair, "token_far")
        results.append(experts(level, [2 * k - 1, 2 * k]))
    pair = both(pair, *(r[-1] for r in results[:-1]), results[-1][0])
    far = experts([jnp.concatenate(pair, axis=0)], [ring.chips - 1])

    total = add(*far)
    pair = forward_far([total, total], "sum_far")
    rows = queries.shape[0]
    for k in range(ring.far - 1, 0, -1):
        behind, ahead, back = results[k]
        up, down = pair
        if k == ring.far - 1:
            zero = jnp.zeros_like(up)
            up = jnp.concatenate([up, zero], axis=0)
            down = jnp.concatenate([zero, down], axis=0)
        up = add(after(ahead, total), back[rows:], up)
        total = add(after(behind, up), back[:rows], down)
        pair = forward([up, total], "sum_" + str(k))
    mine, back = results[0]
    mixed = add(hidden, mine, back, *pair)
    return projected, mixed


def exchange_body(
    n,
    queries,
    keys,
    values,
    block_ids,
    out_weight,
    summary_gain,
    norm_gain,
    routes,
    route_scores,
    expert_gate,
    expert_up,
    expert_down,
):
    tokens_here = queries.shape[0]
    index = lax.axis_index("ctx")
    small = summarize(block_ids, keys, values, summary_gain, routes, route_scores, 0)
    small = lax.all_gather(small, "ctx", axis=0, tiled=False)
    attended = attend(jnp.stack([index, 0 * index]), queries, keys, values, small)
    hidden = jnp.dot(
        attended,
        lax.all_gather(out_weight, "ctx", axis=0, tiled=True),
        preferred_element_type=F32,
    )
    normed = (normalize(hidden) * norm_gain).astype(BF16)
    combine = route_scores / jnp.sum(route_scores, axis=-1, keepdims=True)
    held = expert_gate.shape[0]
    experts_all = held * n
    capacity = capacity_of(tokens_here, experts_all)
    flat_routes = routes.reshape(-1)
    count = tokens_here * TOP
    hits = flat_routes[:, None] == jnp.arange(experts_all, dtype=jnp.int32)[None, :]
    before = jnp.arange(count)[:, None] > jnp.arange(count)[None, :]
    ahead = jnp.dot(before.astype(BF16), hits.astype(BF16), preferred_element_type=F32)
    slot = jnp.sum(jnp.where(hits, ahead, 0.0), axis=-1).astype(jnp.int32)
    target = flat_routes * capacity + slot
    source = jnp.arange(count, dtype=jnp.int32) // TOP
    outgoing = jnp.zeros((experts_all * capacity, D), BF16).at[target].set(normed[source])
    outgoing = outgoing.reshape(experts_all, capacity, D)
    arrived = lax.all_to_all(outgoing, "ctx", split_axis=0, concat_axis=0, tiled=True)
    inputs = (
        arrived.reshape(n, held, capacity, D).transpose(1, 0, 2, 3).reshape(held, n * capacity, D)
    )
    gate = jnp.einsum("erd,edf->erf", inputs, expert_gate, preferred_element_type=F32)
    upper = jnp.einsum("erd,edf->erf", inputs, expert_up, preferred_element_type=F32)
    act = (jax.nn.silu(gate) * upper).astype(BF16)
    result = jnp.einsum("erf,efd->erd", act, expert_down, preferred_element_type=F32)
    result = (
        result.astype(BF16)
        .reshape(held, n, capacity, D)
        .transpose(1, 0, 2, 3)
        .reshape(n * held, capacity, D)
    )
    returned = lax.all_to_all(result, "ctx", split_axis=0, concat_axis=0, tiled=True)
    returned = returned.reshape(experts_all * capacity, D)
    picked = jnp.take(returned, target, axis=0).reshape(tokens_here, TOP, D)
    blended = jnp.sum(combine[:, :, None] * picked.astype(F32), axis=1)
    return (hidden.astype(BF16), (hidden + blended).astype(BF16))


def capacity_of(tokens, experts):
    return max(2, 5 * tokens * TOP // (4 * experts))


def solution(mesh):
    n = mesh.shape["ctx"]

    def body(*args):
        tokens, held = args[0].shape[0], args[9].shape[0]
        dense = tokens <= 2 * capacity_of(tokens, held * n) and held == 1
        fits = n >= 16 and n & (n - 1) == 0
        return (ring_body if dense and fits else exchange_body)(n, *args)

    in_specs = (
        P(("groups", "ctx"), None),
        P(("groups", "ctx"), None),
        P(("groups", "ctx"), None),
        P(("groups", "ctx")),
        P("ctx", None),
        P(),
        P(),
        P(("groups", "ctx"), None),
        P(("groups", "ctx"), None),
        P("ctx", None, None),
        P("ctx", None, None),
        P("ctx", None, None),
    )
    out_specs = (P(("groups", "ctx"), None), P(("groups", "ctx"), None))
    return jax.shard_map(body, mesh=mesh, in_specs=in_specs, out_specs=out_specs, check_vma=False)
```

```python
import functools
import math

import jax
import jax.numpy as jnp
from jax import lax
from jax.experimental import pallas as pl
from jax.experimental.pallas import tpu as pltpu
from jax.sharding import PartitionSpec as P

D = 2048
HQ = 16
KVH = 4
HD = 128
TOP = 8
NB = 4
CORES = 2
VMEM_BYTES = 16 * 1024 * 1024
F32 = jnp.float32
BF16 = jnp.bfloat16


def normalize(x):
    return x * lax.rsqrt(jnp.mean(x * x, axis=-1, keepdims=True) + 1e-06)


def params(size=VMEM_BYTES):
    return pltpu.CompilerParams(vmem_limit_bytes=size)


def smem():
    return pl.BlockSpec(memory_space=pltpu.SMEM)


def vmem():
    return pl.BlockSpec(memory_space=pltpu.VMEM)


def hbm():
    return pl.BlockSpec(memory_space=pltpu.HBM)


def load(sources, targets, arrived):
    copies = [
        pltpu.make_async_copy(source, target, arrived.at[i])
        for i, (source, target) in enumerate(zip(sources, targets))
    ]
    for copy in copies:
        copy.start()
    for copy in copies:
        copy.wait()


def landing(arrays):
    return [pltpu.VMEM(a.shape, a.dtype) for a in arrays] + [
        pltpu.SemaphoreType.DMA((len(arrays),))
    ]


def summary_kernel(experts, *refs):
    sources, out, rows = refs[:6], refs[6], refs[7]
    ids, keys, values, gain, routes, scores, arrived = refs[8:]
    load(sources, (ids, keys, values, gain, routes, scores), arrived)
    tokens = ids.shape[1]
    block = lax.broadcasted_iota(jnp.int32, (8, tokens), 0)
    member = (ids[...] == block) & (block < NB)
    ones = jnp.where(member, 1.0, 0.0).astype(F32)
    count = jnp.maximum(jnp.sum(ones, axis=-1, keepdims=True), 1.0)
    indicator = ones.astype(BF16)
    kmean = jnp.dot(indicator, keys[...], preferred_element_type=F32) / count
    vmean = jnp.dot(indicator, values[...], preferred_element_type=F32) / count
    for g in range(KVH):
        cols = slice(g * HD, (g + 1) * HD)
        rows[8 * g : 8 * g + NB, :] = (normalize(kmean[:, cols]) * gain[...])[:NB]
        rows[8 * g + NB : 8 * g + 2 * NB, :] = normalize(vmean[:, cols])[:NB]
    base = 8 * KVH
    if experts:
        combine = scores[...] / jnp.sum(scores[...], axis=0, keepdims=True)
        expert = lax.broadcasted_iota(jnp.int32, (experts, tokens), 0)
        table = jnp.zeros((experts, tokens), F32)
        for k in range(TOP):
            table += jnp.where(routes[k : k + 1, :] == expert, combine[k : k + 1, :], 0.0)
        high = table.astype(BF16).astype(F32)
        rows[base : base + experts, :] = high
        rows[base + experts : base + 2 * experts, :] = table - high
    out[...] = rows[...].astype(BF16)


def summarize(ids, keys, values, gain, routes, scores, experts):
    tokens = ids.shape[0]
    height = 8 * KVH + 2 * experts
    arrays = (ids.reshape(1, tokens), keys, values, gain.reshape(1, HD), routes.T, scores.T)
    return pl.pallas_call(
        functools.partial(summary_kernel, experts),
        in_specs=[hbm()] * 6,
        out_specs=vmem(),
        out_shape=jax.ShapeDtypeStruct((height, HD), BF16),
        scratch_shapes=[pltpu.VMEM((height, HD), F32), *landing(arrays)],
        compiler_params=params(60 * 1024 * 1024),
        name="summaries",
    )(*arrays)


def attention_kernel(me, owners, gathered, *refs):
    sources, attended = refs[:3], refs[3]
    queries, keys, values, arrived = refs[4:]
    load(sources, (queries, keys, values), arrived)
    tokens = queries.shape[0]
    group = HQ // KVH
    scale = 1.0 / math.sqrt(HD)
    shards = gathered.shape[0]
    wide = shards * 2 * NB
    row = lax.broadcasted_iota(jnp.int32, (tokens, tokens), 0)
    col = lax.broadcasted_iota(jnp.int32, (tokens, tokens), 1)
    causal = row >= col
    place = lax.broadcasted_iota(jnp.int32, (tokens, wide), 1)
    earlier = (owners[...] < me[0]) & (place % (2 * NB) < NB)
    seen = jnp.concatenate([causal, earlier], axis=1)
    for g in range(KVH):
        cols = slice(g * HD, (g + 1) * HD)
        pairs = gathered[:, 16 * (g // 2) : 16 * (g // 2) + 16, :].astype(F32)
        half = 8 * (g % 2)
        remote = pairs[:, half : half + 8, :].reshape(wide, HD)
        key_all = jnp.concatenate([keys[:, cols], remote.astype(BF16)], axis=0)
        shifted = pltpu.roll(remote, wide - NB, 0)
        value_all = jnp.concatenate([values[:, cols], shifted.astype(BF16)], axis=0)
        for i in range(group):
            h = g * group + i
            head = slice(h * HD, (h + 1) * HD)
            scores = (
                lax.dot_general(
                    queries[:, head],
                    key_all,
                    (((1,), (1,)), ((), ())),
                    preferred_element_type=F32,
                )
                * scale
            )
            scores = jnp.where(seen, scores, -jnp.inf)
            top = jnp.max(scores, axis=-1, keepdims=True)
            expo = jnp.exp(scores - top)
            weights = (expo / jnp.sum(expo, axis=-1, keepdims=True)).astype(BF16)
            attended[:, head] = jnp.dot(
                weights, value_all, preferred_element_type=F32
            ).astype(BF16)


def attend(index, shards, queries, keys, values, gathered):
    tokens = queries.shape[0]
    owners = jnp.repeat(shards, 2 * NB).reshape(1, -1)
    return pl.pallas_call(
        attention_kernel,
        in_specs=[smem(), vmem(), vmem()] + [hbm()] * 3,
        out_specs=vmem(),
        out_shape=jax.ShapeDtypeStruct((tokens, HQ * HD), BF16),
        scratch_shapes=landing((queries, keys, values)),
        compiler_params=params(56 * 1024 * 1024),
        cost_estimate=pl.CostEstimate(
            flops=4 * HQ * HD * tokens * 2 * tokens,
            bytes_accessed=2 * 4 * tokens * HQ * HD,
            transcendentals=HQ * tokens * 2 * tokens,
        ),
        name="attention",
    )(index.reshape(1), owners, gathered, queries, keys, values)


def pair_up(here, pair, own, other):
    rows = pair.shape[0] // CORES
    at = pl.multiple_of(here[0] * rows, rows)
    for i, block in enumerate(own):
        step = i * block.shape[0]
        pair[pl.ds(at + step, block.shape[0]), :] = block[...]
    at = pl.multiple_of((1 - here[0]) * rows, rows)
    for i, block in enumerate(other):
        step = i * block.shape[0]
        pair[pl.ds(at + step, block.shape[0]), :] = block[...]


def project_first_kernel(levels, here, tokens, *refs):
    blocks, acc, pair = refs[:-2], refs[-2], refs[-1]
    rows = pair.shape[1]
    for i in range(levels):
        pair_up(here, pair.at[i], [blocks[2 * i]], [blocks[2 * i + 1]])
    for i in range(levels):
        at = pl.multiple_of(here[1 + i] * rows, rows)
        part = jnp.dot(tokens[:, pl.ds(at, rows)], pair[i], preferred_element_type=F32)
        if i == 0:
            acc[...] = part
        else:
            acc[...] += part


def project_first(here, tokens, blocks):
    rows, width = blocks[0].shape
    levels = len(blocks) // 2
    return pl.pallas_call(
        functools.partial(project_first_kernel, levels),
        in_specs=[smem()] + [vmem()] * (1 + len(blocks)),
        out_specs=vmem(),
        out_shape=jax.ShapeDtypeStruct((tokens.shape[0], width), F32),
        scratch_shapes=[pltpu.VMEM((levels, 2 * rows, width), BF16)],
        compiler_params=params(),
        cost_estimate=pl.CostEstimate(
            flops=2 * tokens.shape[0] * rows * width * len(blocks),
            bytes_accessed=2 * rows * width * len(blocks),
            transcendentals=0,
        ),
        name="project_first",
    )(here, tokens, *blocks)


def project_last_kernel(at, here, tokens, acc, gain, a, b, c, d, hidden, projected, normed, pair):
    rows = pair.shape[0]
    pair_up(here, pair, [a, b], [c, d])
    columns = pl.ds(pl.multiple_of(here[at] * rows, rows), rows)
    total = acc[...] + jnp.dot(tokens[:, columns], pair[...], preferred_element_type=F32)
    hidden[...] = total
    projected[...] = total.astype(BF16)
    normed[...] = (normalize(total) * gain[...]).astype(BF16)


def project_last(at, here, tokens, acc, gain, halves):
    count, width = acc.shape
    half = halves[0].shape[0]
    return pl.pallas_call(
        functools.partial(project_last_kernel, at),
        in_specs=[smem()] + [vmem()] * 7,
        out_specs=[vmem()] * 3,
        out_shape=[
            jax.ShapeDtypeStruct((count, width), F32),
            jax.ShapeDtypeStruct((count, width), BF16),
            jax.ShapeDtypeStruct((count, width), BF16),
        ],
        scratch_shapes=[pltpu.VMEM((4 * half, width), BF16)],
        compiler_params=params(),
        cost_estimate=pl.CostEstimate(
            flops=8 * count * half * width, bytes_accessed=12 * count * width, transcendentals=0
        ),
        name="project_last",
    )(here, tokens, acc, gain.reshape(1, width), *halves)


def expert_kernel(places, here, table, *refs):
    count = len(places)
    own = count // 2
    blocks, (gate, up, down) = refs[:count], refs[count : count + 3]
    outs = refs[count + 3 : count + 3 + own]
    sent = refs[count + 3 + own]
    tokens, act, scale = refs[count + 4 + own :]
    rows, depth = blocks[0].shape
    lanes = table.shape[1]
    ff = gate.shape[2]
    tile = 256
    for i in range(count):
        tokens[i * rows : (i + 1) * rows, :] = blocks[i][...]
        weight = table[pl.ds(here[places[i]], 1), :]
        weight = jnp.transpose(jnp.broadcast_to(weight, (lanes, lanes)))
        scale[i * rows : (i + 1) * rows, :] = weight
    for f in range(0, ff, tile):
        cols = slice(f, f + tile)
        g = jnp.dot(tokens[...], gate[0, :, cols], preferred_element_type=F32)
        u = jnp.dot(tokens[...], up[0, :, cols], preferred_element_type=F32)
        act[:, cols] = (g / (1.0 + jnp.exp(-g)) * u).astype(BF16)
    for d in range(0, depth, tile):
        cols = slice(d, d + tile)
        part = jnp.dot(act[...], down[0, :, cols], preferred_element_type=F32)
        weight = jnp.concatenate([scale[...]] * (tile // lanes), axis=1)
        part = (part * weight).astype(BF16)
        for i in range(own):
            outs[i][:, cols] = part[i * rows : (i + 1) * rows]
        sent[:, cols] = part[own * rows :]


def expert_blocks(places, here, table, blocks, gate, up, down):
    count = len(blocks)
    own = count // 2
    rows, width = blocks[0].shape
    ff = gate.shape[2]
    return pl.pallas_call(
        functools.partial(expert_kernel, places),
        in_specs=[smem()] + [vmem()] * (1 + count + 3),
        out_specs=[vmem()] * (own + 1),
        out_shape=[jax.ShapeDtypeStruct((rows, width), BF16)] * own
        + [jax.ShapeDtypeStruct((own * rows, width), BF16)],
        scratch_shapes=[
            pltpu.VMEM((count * rows, width), BF16),
            pltpu.VMEM((count * rows, ff), BF16),
            pltpu.VMEM((count * rows, table.shape[1]), F32),
        ],
        compiler_params=params(),
        cost_estimate=pl.CostEstimate(flops=0, bytes_accessed=0, transcendentals=0),
        name="experts",
    )(here, table, *blocks, gate, up, down)


class Ring:
    def __init__(self, n):
        self.chips = n // CORES
        self.cycle = [*range(0, self.chips, 2), *range(self.chips - 1, 0, -2)]
        self.far = self.chips // 2

    def step(self, x, by, label):
        pairs = []
        for p, chip in enumerate(self.cycle):
            to = self.cycle[(p + by) % self.chips]
            pairs += [(chip * CORES + c, to * CORES + c) for c in range(CORES)]
        with jax.named_scope(label + ("_up" if by > 0 else "_down")):
            return lax.ppermute(x, "ctx", pairs)

    def swap(self, x):
        n = self.chips * CORES
        with jax.named_scope("swap_cores"):
            return lax.ppermute(x, "ctx", [(i, i ^ 1) for i in range(n)])

    def table(self, n, order):
        place = {chip: p for p, chip in enumerate(self.cycle)}
        rows = []
        for i in range(n):
            p, core = place[i // CORES], i % CORES
            chips = [self.cycle[p]]
            for k in range(1, self.far):
                chips += [self.cycle[(p - k) % self.chips], self.cycle[(p + k) % self.chips]]
            chips.append(self.cycle[(p + self.far) % self.chips])
            own = [order.index((chip * CORES + core) ^ i) for chip in chips]
            other = [order.index((chip * CORES + 1 - core) ^ i) for chip in chips]
            rows.append([core, *chips, *own, *other])
        return rows


def xor_round(x, order, masks, n):
    with jax.named_scope("summary_round"):
        others = [lax.ppermute(x, "ctx", [(i, i ^ mask) for i in range(n)]) for mask in masks]
    return jnp.concatenate([x, *others], axis=0), [o ^ m for m in (0, *masks) for o in order]


def after(x, *earlier):
    return lax.optimization_barrier((x, earlier))[0]


def add(*xs):
    total = xs[0].astype(F32)
    for x in xs[1:]:
        total = total + x.astype(F32)
    return total.astype(BF16)


def ring_body(
    n,
    queries,
    keys,
    values,
    block_ids,
    out_weight,
    summary_gain,
    norm_gain,
    routes,
    route_scores,
    expert_gate,
    expert_up,
    expert_down,
):
    index = lax.axis_index("ctx")
    core = index % CORES
    ring = Ring(n)
    half = queries.shape[0] // 2

    def both(pair, *earlier):
        return [after(x, *earlier) for x in pair]

    def forward(pair, label):
        return [ring.step(pair[0], 1, label), ring.step(pair[1], -1, label)]

    def forward_far(pair, label):
        return forward([pair[0][:half], pair[1][half:]], label)

    pair = forward([out_weight, out_weight], "weight_1")
    blocks = [out_weight, ring.swap(out_weight)]
    small = summarize(block_ids, keys, values, summary_gain, routes, route_scores, n)[None]
    small, order = xor_round(small, [0], [1], n)
    for bit in range(n.bit_length() - 2, 2, -1):
        small, order = xor_round(small, order, [1 << bit], n)
    for k in range(1, ring.far):
        if k == 1:
            small = after(small, *pair)
            small, order = xor_round(small, order, [2, 4, 6], n)
            shards = jnp.asarray(order, jnp.int32) ^ index
            here = jnp.asarray(ring.table(n, order), jnp.int32)[index]
            attended = attend(index, shards, queries, keys, values, small[:, : 8 * KVH])
        if k == 2:
            pair = both(pair, attended)
        for x in pair:
            blocks += [x, ring.swap(x)]
        if k < ring.far - 1:
            pair = forward(pair, "weight_" + str(k + 1))
    pair = forward_far(pair, "weight_far")
    base = 8 * KVH
    parts = lax.dynamic_index_in_dim(
        small[:, base:].reshape(n, 2, n, HD), index, axis=2, keepdims=False
    ).astype(F32)
    table = parts[:, 0] + parts[:, 1]
    acc = project_first(here, attended, blocks)
    pair = both(pair, acc, table)
    hidden, projected, normed = project_last(
        ring.chips, here, attended, acc, norm_gain, [*pair, *(ring.swap(x) for x in pair)]
    )

    def experts(level, chips):
        others = [ring.swap(x) for x in level]
        places = [1 + ring.chips + c for c in chips] + [1 + 2 * ring.chips + c for c in chips]
        *kept, sent = expert_blocks(
            tuple(places), here, table, [*level, *others], expert_gate, expert_up, expert_down
        )
        return [*kept, ring.swap(sent)]

    pair = forward([normed, normed], "token_1")
    results = [experts([normed], [0])]
    for k in range(1, ring.far):
        pair = both(pair, results[-1][0])
        level = pair
        if k < ring.far - 1:
            pair = forward(pair, "token_" + str(k + 1))
        else:
            pair = forward_far(pair, "token_far")
        results.append(experts(level, [2 * k - 1, 2 * k]))
    pair = both(pair, *(r[-1] for r in results[:-1]), results[-1][0])
    far = experts([jnp.concatenate(pair, axis=0)], [ring.chips - 1])

    total = add(*far)
    pair = forward_far([total, total], "sum_far")
    rows = queries.shape[0]
    for k in range(ring.far - 1, 0, -1):
        behind, ahead, back = results[k]
        up, down = pair
        if k == ring.far - 1:
            zero = jnp.zeros_like(up)
            up = jnp.concatenate([up, zero], axis=0)
            down = jnp.concatenate([zero, down], axis=0)
        up = add(after(ahead, total), back[rows:], up)
        total = add(after(behind, up), back[:rows], down)
        pair = forward([up, total], "sum_" + str(k))
    mine, back = results[0]
    mixed = add(hidden, mine, back, *pair)
    return projected, mixed


def exchange_body(
    n,
    queries,
    keys,
    values,
    block_ids,
    out_weight,
    summary_gain,
    norm_gain,
    routes,
    route_scores,
    expert_gate,
    expert_up,
    expert_down,
):
    tokens_here = queries.shape[0]
    index = lax.axis_index("ctx")
    small = summarize(block_ids, keys, values, summary_gain, routes, route_scores, 0)
    small = lax.all_gather(small, "ctx", axis=0, tiled=False)
    shards = jnp.arange(n, dtype=jnp.int32)
    attended = attend(index, shards, queries, keys, values, small)
    hidden = jnp.dot(
        attended,
        lax.all_gather(out_weight, "ctx", axis=0, tiled=True),
        preferred_element_type=F32,
    )
    normed = (normalize(hidden) * norm_gain).astype(BF16)
    combine = route_scores / jnp.sum(route_scores, axis=-1, keepdims=True)
    held = expert_gate.shape[0]
    experts_all = held * n
    capacity = capacity_of(tokens_here, experts_all)
    flat_routes = routes.reshape(-1)
    count = tokens_here * TOP
    hits = flat_routes[:, None] == jnp.arange(experts_all, dtype=jnp.int32)[None, :]
    before = jnp.arange(count)[:, None] > jnp.arange(count)[None, :]
    ahead = jnp.dot(before.astype(BF16), hits.astype(BF16), preferred_element_type=F32)
    slot = jnp.sum(jnp.where(hits, ahead, 0.0), axis=-1).astype(jnp.int32)
    target = flat_routes * capacity + slot
    source = jnp.arange(count, dtype=jnp.int32) // TOP
    outgoing = jnp.zeros((experts_all * capacity, D), BF16).at[target].set(normed[source])
    outgoing = outgoing.reshape(experts_all, capacity, D)
    arrived = lax.all_to_all(outgoing, "ctx", split_axis=0, concat_axis=0, tiled=True)
    inputs = (
        arrived.reshape(n, held, capacity, D).transpose(1, 0, 2, 3).reshape(held, n * capacity, D)
    )
    gate = jnp.einsum("erd,edf->erf", inputs, expert_gate, preferred_element_type=F32)
    upper = jnp.einsum("erd,edf->erf", inputs, expert_up, preferred_element_type=F32)
    act = (jax.nn.silu(gate) * upper).astype(BF16)
    result = jnp.einsum("erf,efd->erd", act, expert_down, preferred_element_type=F32)
    result = (
        result.astype(BF16)
        .reshape(held, n, capacity, D)
        .transpose(1, 0, 2, 3)
        .reshape(n * held, capacity, D)
    )
    returned = lax.all_to_all(result, "ctx", split_axis=0, concat_axis=0, tiled=True)
    returned = returned.reshape(experts_all * capacity, D)
    picked = jnp.take(returned, target, axis=0).reshape(tokens_here, TOP, D)
    blended = jnp.sum(combine[:, :, None] * picked.astype(F32), axis=1)
    return (hidden.astype(BF16), (hidden + blended).astype(BF16))


def capacity_of(tokens, experts):
    return max(2, 5 * tokens * TOP // (4 * experts))


def solution(mesh):
    n = mesh.shape["ctx"]

    def body(*args):
        tokens, held = args[0].shape[0], args[9].shape[0]
        dense = tokens <= 2 * capacity_of(tokens, held * n) and held == 1
        fits = n >= 16 and n & (n - 1) == 0
        return (ring_body if dense and fits else exchange_body)(n, *args)

    in_specs = (
        P(("groups", "ctx"), None),
        P(("groups", "ctx"), None),
        P(("groups", "ctx"), None),
        P(("groups", "ctx")),
        P("ctx", None),
        P(),
        P(),
        P(("groups", "ctx"), None),
        P(("groups", "ctx"), None),
        P("ctx", None, None),
        P("ctx", None, None),
        P("ctx", None, None),
    )
    out_specs = (P(("groups", "ctx"), None), P(("groups", "ctx"), None))
    return jax.shard_map(body, mesh=mesh, in_specs=in_specs, out_specs=out_specs, check_vma=False)
```

```python
import functools
import math

import jax
import jax.numpy as jnp
from jax import lax
from jax.experimental import pallas as pl
from jax.experimental.pallas import tpu as pltpu
from jax.sharding import PartitionSpec as P

D = 2048
HQ = 16
KVH = 4
HD = 128
TOP = 8
NB = 4
CORES = 2
VMEM_BYTES = 16 * 1024 * 1024
F32 = jnp.float32
BF16 = jnp.bfloat16


def normalize(x):
    return x * lax.rsqrt(jnp.mean(x * x, axis=-1, keepdims=True) + 1e-06)


def params(size=VMEM_BYTES):
    return pltpu.CompilerParams(vmem_limit_bytes=size)


def smem():
    return pl.BlockSpec(memory_space=pltpu.SMEM)


def vmem():
    return pl.BlockSpec(memory_space=pltpu.VMEM)


def hbm():
    return pl.BlockSpec(memory_space=pltpu.HBM)


def load(sources, targets, arrived):
    copies = [
        pltpu.make_async_copy(source, target, arrived.at[i])
        for i, (source, target) in enumerate(zip(sources, targets))
    ]
    for copy in copies:
        copy.start()
    for copy in copies:
        copy.wait()


def landing(arrays):
    return [pltpu.VMEM(a.shape, a.dtype) for a in arrays] + [
        pltpu.SemaphoreType.DMA((len(arrays),))
    ]


def summary_kernel(experts, *refs):
    sources, out, rows = refs[:6], refs[6], refs[7]
    ids, keys, values, gain, routes, scores, arrived = refs[8:]
    load(sources, (ids, keys, values, gain, routes, scores), arrived)
    tokens = ids.shape[1]
    block = lax.broadcasted_iota(jnp.int32, (8, tokens), 0)
    member = (ids[...] == block) & (block < NB)
    ones = jnp.where(member, 1.0, 0.0).astype(F32)
    count = jnp.maximum(jnp.sum(ones, axis=-1, keepdims=True), 1.0)
    indicator = ones.astype(BF16)
    kmean = jnp.dot(indicator, keys[...], preferred_element_type=F32) / count
    vmean = jnp.dot(indicator, values[...], preferred_element_type=F32) / count
    for g in range(KVH):
        cols = slice(g * HD, (g + 1) * HD)
        rows[8 * g : 8 * g + NB, :] = (normalize(kmean[:, cols]) * gain[...])[:NB]
        rows[8 * g + NB : 8 * g + 2 * NB, :] = normalize(vmean[:, cols])[:NB]
    base = 8 * KVH
    if experts:
        combine = scores[...] / jnp.sum(scores[...], axis=0, keepdims=True)
        expert = lax.broadcasted_iota(jnp.int32, (experts, tokens), 0)
        table = jnp.zeros((experts, tokens), F32)
        for k in range(TOP):
            table += jnp.where(routes[k : k + 1, :] == expert, combine[k : k + 1, :], 0.0)
        high = table.astype(BF16).astype(F32)
        rows[base : base + experts, :] = high
        rows[base + experts : base + 2 * experts, :] = table - high
    out[...] = rows[...].astype(BF16)


def summarize(ids, keys, values, gain, routes, scores, experts):
    tokens = ids.shape[0]
    height = 8 * KVH + 2 * experts
    arrays = (ids.reshape(1, tokens), keys, values, gain.reshape(1, HD), routes.T, scores.T)
    return pl.pallas_call(
        functools.partial(summary_kernel, experts),
        in_specs=[hbm()] * 6,
        out_specs=vmem(),
        out_shape=jax.ShapeDtypeStruct((height, HD), BF16),
        scratch_shapes=[pltpu.VMEM((height, HD), F32), *landing(arrays)],
        compiler_params=params(60 * 1024 * 1024),
        name="summaries",
    )(*arrays)


def attention_kernel(me, owners, gathered, *refs):
    sources, attended = refs[:3], refs[3]
    queries, keys, values, arrived = refs[4:]
    load(sources, (queries, keys, values), arrived)
    tokens = queries.shape[0]
    group = HQ // KVH
    scale = 1.0 / math.sqrt(HD)
    shards = gathered.shape[0]
    wide = shards * 2 * NB
    row = lax.broadcasted_iota(jnp.int32, (tokens, tokens), 0)
    col = lax.broadcasted_iota(jnp.int32, (tokens, tokens), 1)
    causal = row >= col
    place = lax.broadcasted_iota(jnp.int32, (tokens, wide), 1)
    earlier = (owners[...] < me[0]) & (place % (2 * NB) < NB)
    seen = jnp.concatenate([causal, earlier], axis=1)
    for g in range(KVH):
        cols = slice(g * HD, (g + 1) * HD)
        pairs = gathered[:, 16 * (g // 2) : 16 * (g // 2) + 16, :].astype(F32)
        half = 8 * (g % 2)
        remote = pairs[:, half : half + 8, :].reshape(wide, HD)
        key_all = jnp.concatenate([keys[:, cols], remote.astype(BF16)], axis=0)
        shifted = pltpu.roll(remote, wide - NB, 0)
        value_all = jnp.concatenate([values[:, cols], shifted.astype(BF16)], axis=0)
        for i in range(group):
            h = g * group + i
            head = slice(h * HD, (h + 1) * HD)
            scores = (
                lax.dot_general(
                    queries[:, head],
                    key_all,
                    (((1,), (1,)), ((), ())),
                    preferred_element_type=F32,
                )
                * scale
            )
            scores = jnp.where(seen, scores, -jnp.inf)
            top = jnp.max(scores, axis=-1, keepdims=True)
            expo = jnp.exp(scores - top)
            weights = (expo / jnp.sum(expo, axis=-1, keepdims=True)).astype(BF16)
            attended[:, head] = jnp.dot(
                weights, value_all, preferred_element_type=F32
            ).astype(BF16)


def attend(index, shards, queries, keys, values, gathered):
    tokens = queries.shape[0]
    owners = jnp.repeat(shards, 2 * NB).reshape(1, -1)
    return pl.pallas_call(
        attention_kernel,
        in_specs=[smem(), vmem(), vmem()] + [hbm()] * 3,
        out_specs=vmem(),
        out_shape=jax.ShapeDtypeStruct((tokens, HQ * HD), BF16),
        scratch_shapes=landing((queries, keys, values)),
        compiler_params=params(56 * 1024 * 1024),
        cost_estimate=pl.CostEstimate(
            flops=4 * HQ * HD * tokens * 2 * tokens,
            bytes_accessed=2 * 4 * tokens * HQ * HD,
            transcendentals=HQ * tokens * 2 * tokens,
        ),
        name="attention",
    )(index.reshape(1), owners, gathered, queries, keys, values)


def pair_up(here, pair, own, other):
    rows = pair.shape[0] // CORES
    at = pl.multiple_of(here[0] * rows, rows)
    for i, block in enumerate(own):
        step = i * block.shape[0]
        pair[pl.ds(at + step, block.shape[0]), :] = block[...]
    at = pl.multiple_of((1 - here[0]) * rows, rows)
    for i, block in enumerate(other):
        step = i * block.shape[0]
        pair[pl.ds(at + step, block.shape[0]), :] = block[...]


def project_first_kernel(levels, here, tokens, *refs):
    blocks, acc, pair = refs[:-2], refs[-2], refs[-1]
    rows = pair.shape[1]
    for i in range(levels):
        pair_up(here, pair.at[i], [blocks[2 * i]], [blocks[2 * i + 1]])
    for i in range(levels):
        at = pl.multiple_of(here[1 + i] * rows, rows)
        part = jnp.dot(tokens[:, pl.ds(at, rows)], pair[i], preferred_element_type=F32)
        if i == 0:
            acc[...] = part
        else:
            acc[...] += part


def project_first(here, tokens, blocks):
    rows, width = blocks[0].shape
    levels = len(blocks) // 2
    return pl.pallas_call(
        functools.partial(project_first_kernel, levels),
        in_specs=[smem()] + [vmem()] * (1 + len(blocks)),
        out_specs=vmem(),
        out_shape=jax.ShapeDtypeStruct((tokens.shape[0], width), F32),
        scratch_shapes=[pltpu.VMEM((levels, 2 * rows, width), BF16)],
        compiler_params=params(),
        cost_estimate=pl.CostEstimate(
            flops=2 * tokens.shape[0] * rows * width * len(blocks),
            bytes_accessed=2 * rows * width * len(blocks),
            transcendentals=0,
        ),
        name="project_first",
    )(here, tokens, *blocks)


def project_last_kernel(at, here, tokens, acc, gain, a, b, c, d, hidden, projected, normed, pair):
    rows = pair.shape[0]
    pair_up(here, pair, [a, b], [c, d])
    columns = pl.ds(pl.multiple_of(here[at] * rows, rows), rows)
    total = acc[...] + jnp.dot(tokens[:, columns], pair[...], preferred_element_type=F32)
    hidden[...] = total
    projected[...] = total.astype(BF16)
    normed[...] = (normalize(total) * gain[...]).astype(BF16)


def project_last(at, here, tokens, acc, gain, halves):
    count, width = acc.shape
    half = halves[0].shape[0]
    return pl.pallas_call(
        functools.partial(project_last_kernel, at),
        in_specs=[smem()] + [vmem()] * 7,
        out_specs=[vmem()] * 3,
        out_shape=[
            jax.ShapeDtypeStruct((count, width), F32),
            jax.ShapeDtypeStruct((count, width), BF16),
            jax.ShapeDtypeStruct((count, width), BF16),
        ],
        scratch_shapes=[pltpu.VMEM((4 * half, width), BF16)],
        compiler_params=params(),
        cost_estimate=pl.CostEstimate(
            flops=8 * count * half * width, bytes_accessed=12 * count * width, transcendentals=0
        ),
        name="project_last",
    )(here, tokens, acc, gain.reshape(1, width), *halves)


def expert_kernel(places, here, table, *refs):
    count = len(places)
    own = count // 2
    blocks, (gate, up, down) = refs[:count], refs[count : count + 3]
    outs = refs[count + 3 : count + 3 + own]
    sent = refs[count + 3 + own]
    tokens, act, scale = refs[count + 4 + own :]
    rows, depth = blocks[0].shape
    lanes = table.shape[1]
    ff = gate.shape[2]
    tile = 256
    for i in range(count):
        tokens[i * rows : (i + 1) * rows, :] = blocks[i][...]
        weight = table[pl.ds(here[places[i][0]], 1), :]
        weight = jnp.transpose(jnp.broadcast_to(weight, (lanes, lanes)))
        scale[i * rows : (i + 1) * rows, :] = weight[places[i][1] : places[i][1] + rows]
    for f in range(0, ff, tile):
        cols = slice(f, f + tile)
        g = jnp.dot(tokens[...], gate[0, :, cols], preferred_element_type=F32)
        u = jnp.dot(tokens[...], up[0, :, cols], preferred_element_type=F32)
        act[:, cols] = (g / (1.0 + jnp.exp(-g)) * u).astype(BF16)
    for d in range(0, depth, tile):
        cols = slice(d, d + tile)
        part = jnp.dot(act[...], down[0, :, cols], preferred_element_type=F32)
        weight = jnp.concatenate([scale[...]] * (tile // lanes), axis=1)
        part = (part * weight).astype(BF16)
        for i in range(own):
            outs[i][:, cols] = part[i * rows : (i + 1) * rows]
        sent[:, cols] = part[own * rows :]


def expert_blocks(places, here, table, blocks, gate, up, down):
    count = len(blocks)
    own = count // 2
    rows, width = blocks[0].shape
    ff = gate.shape[2]
    return pl.pallas_call(
        functools.partial(expert_kernel, places),
        in_specs=[smem()] + [vmem()] * (1 + count + 3),
        out_specs=[vmem()] * (own + 1),
        out_shape=[jax.ShapeDtypeStruct((rows, width), BF16)] * own
        + [jax.ShapeDtypeStruct((own * rows, width), BF16)],
        scratch_shapes=[
            pltpu.VMEM((count * rows, width), BF16),
            pltpu.VMEM((count * rows, ff), BF16),
            pltpu.VMEM((count * rows, table.shape[1]), F32),
        ],
        compiler_params=params(),
        cost_estimate=pl.CostEstimate(flops=0, bytes_accessed=0, transcendentals=0),
        name="experts",
    )(here, table, *blocks, gate, up, down)


class Ring:
    def __init__(self, n):
        self.chips = n // CORES
        self.cycle = [*range(0, self.chips, 2), *range(self.chips - 1, 0, -2)]
        self.far = self.chips // 2

    def step(self, x, by, label):
        pairs = []
        for p, chip in enumerate(self.cycle):
            to = self.cycle[(p + by) % self.chips]
            pairs += [(chip * CORES + c, to * CORES + c) for c in range(CORES)]
        with jax.named_scope(label + ("_up" if by > 0 else "_down")):
            return lax.ppermute(x, "ctx", pairs)

    def swap(self, x):
        n = self.chips * CORES
        with jax.named_scope("swap_cores"):
            return lax.ppermute(x, "ctx", [(i, i ^ 1) for i in range(n)])

    def table(self, n, order):
        place = {chip: p for p, chip in enumerate(self.cycle)}
        rows = []
        for i in range(n):
            p, core = place[i // CORES], i % CORES
            chips = [self.cycle[p]]
            for k in range(1, self.far):
                chips += [self.cycle[(p - k) % self.chips], self.cycle[(p + k) % self.chips]]
            chips.append(self.cycle[(p + self.far) % self.chips])
            own = [order.index((chip * CORES + core) ^ i) for chip in chips]
            other = [order.index((chip * CORES + 1 - core) ^ i) for chip in chips]
            rows.append([core, *chips, *own, *other])
        return rows


def xor_round(x, order, masks, n):
    with jax.named_scope("summary_round"):
        others = [lax.ppermute(x, "ctx", [(i, i ^ mask) for i in range(n)]) for mask in masks]
    return jnp.concatenate([x, *others], axis=0), [o ^ m for m in (0, *masks) for o in order]


def after(x, *earlier):
    return lax.optimization_barrier((x, earlier))[0]


def add(*xs):
    total = xs[0].astype(F32)
    for x in xs[1:]:
        total = total + x.astype(F32)
    return total.astype(BF16)


def ring_body(
    n,
    queries,
    keys,
    values,
    block_ids,
    out_weight,
    summary_gain,
    norm_gain,
    routes,
    route_scores,
    expert_gate,
    expert_up,
    expert_down,
):
    index = lax.axis_index("ctx")
    core = index % CORES
    ring = Ring(n)
    half = queries.shape[0] // 2

    def both(pair, *earlier):
        return [after(x, *earlier) for x in pair]

    def forward(pair, label):
        return [ring.step(pair[0], 1, label), ring.step(pair[1], -1, label)]

    def forward_far(pair, label):
        return forward([pair[0][:half], pair[1][half:]], label)

    pair = forward([out_weight, out_weight], "weight_1")
    blocks = [out_weight, ring.swap(out_weight)]
    small = summarize(block_ids, keys, values, summary_gain, routes, route_scores, n)[None]
    small, order = xor_round(small, [0], [1], n)
    for bit in range(n.bit_length() - 2, 2, -1):
        small, order = xor_round(small, order, [1 << bit], n)
    for k in range(1, ring.far):
        if k == 1:
            small = after(small, *pair)
            small, order = xor_round(small, order, [2, 4, 6], n)
            shards = jnp.asarray(order, jnp.int32) ^ index
            here = jnp.asarray(ring.table(n, order), jnp.int32)[index]
            attended = attend(index, shards, queries, keys, values, small[:, : 8 * KVH])
        if k == 2:
            pair = both(pair, attended)
        for x in pair:
            blocks += [x, ring.swap(x)]
        if k < ring.far - 1:
            pair = forward(pair, "weight_" + str(k + 1))
    pair = forward_far(pair, "weight_far")
    base = 8 * KVH
    parts = lax.dynamic_index_in_dim(
        small[:, base:].reshape(n, 2, n, HD), index, axis=2, keepdims=False
    ).astype(F32)
    table = parts[:, 0] + parts[:, 1]
    acc = project_first(here, attended, blocks)
    pair = both(pair, acc, table)
    hidden, projected, normed = project_last(
        ring.chips, here, attended, acc, norm_gain, [*pair, *(ring.swap(x) for x in pair)]
    )

    def experts(level, chips, firsts=(0, 0)):
        others = [ring.swap(x) for x in level]
        places = [(1 + ring.chips + c, first) for c, first in zip(chips, firsts)]
        places += [(1 + 2 * ring.chips + c, first) for c, first in zip(chips, firsts)]
        *kept, sent = expert_blocks(
            tuple(places), here, table, [*level, *others], expert_gate, expert_up, expert_down
        )
        return [*kept, ring.swap(sent)]

    pair = forward([normed, normed], "token_1")
    results = [[normed]]
    for k in range(1, ring.far):
        if k > 1:
            pair = both(pair, results[-1][0])
        level = pair
        if k < ring.far - 1:
            pair = forward(pair, "token_" + str(k + 1))
        else:
            pair = forward_far(pair, "token_far")
        results.append(experts(level, [2 * k - 1, 2 * k]))
    pair = both(pair, *(r[-1] for r in results[1:-1]), results[-1][0])
    far_up, far_down, back = experts(pair, [ring.chips - 1] * 2, (0, half))

    up = add(far_up, back[:half])
    total = add(after(far_down, up), back[half:])
    pair = forward([up, total], "sum_far")
    results[0] = experts([after(normed, total)], [0])
    rows = queries.shape[0]
    for k in range(ring.far - 1, 0, -1):
        behind, ahead, back = results[k]
        up, down = pair
        if k == ring.far - 1:
            zero = jnp.zeros_like(up)
            up = jnp.concatenate([up, zero], axis=0)
            down = jnp.concatenate([zero, down], axis=0)
        up = add(after(ahead, total), back[rows:], up)
        total = add(after(behind, up), back[:rows], down)
        pair = forward([up, total], "sum_" + str(k))
    mine, back = results[0]
    mixed = add(hidden, mine, back, *pair)
    return projected, mixed


def exchange_body(
    n,
    queries,
    keys,
    values,
    block_ids,
    out_weight,
    summary_gain,
    norm_gain,
    routes,
    route_scores,
    expert_gate,
    expert_up,
    expert_down,
):
    tokens_here = queries.shape[0]
    index = lax.axis_index("ctx")
    small = summarize(block_ids, keys, values, summary_gain, routes, route_scores, 0)
    small = lax.all_gather(small, "ctx", axis=0, tiled=False)
    shards = jnp.arange(n, dtype=jnp.int32)
    attended = attend(index, shards, queries, keys, values, small)
    hidden = jnp.dot(
        attended,
        lax.all_gather(out_weight, "ctx", axis=0, tiled=True),
        preferred_element_type=F32,
    )
    normed = (normalize(hidden) * norm_gain).astype(BF16)
    combine = route_scores / jnp.sum(route_scores, axis=-1, keepdims=True)
    held = expert_gate.shape[0]
    experts_all = held * n
    capacity = capacity_of(tokens_here, experts_all)
    flat_routes = routes.reshape(-1)
    count = tokens_here * TOP
    hits = flat_routes[:, None] == jnp.arange(experts_all, dtype=jnp.int32)[None, :]
    before = jnp.arange(count)[:, None] > jnp.arange(count)[None, :]
    ahead = jnp.dot(before.astype(BF16), hits.astype(BF16), preferred_element_type=F32)
    slot = jnp.sum(jnp.where(hits, ahead, 0.0), axis=-1).astype(jnp.int32)
    target = flat_routes * capacity + slot
    source = jnp.arange(count, dtype=jnp.int32) // TOP
    outgoing = jnp.zeros((experts_all * capacity, D), BF16).at[target].set(normed[source])
    outgoing = outgoing.reshape(experts_all, capacity, D)
    arrived = lax.all_to_all(outgoing, "ctx", split_axis=0, concat_axis=0, tiled=True)
    inputs = (
        arrived.reshape(n, held, capacity, D).transpose(1, 0, 2, 3).reshape(held, n * capacity, D)
    )
    gate = jnp.einsum("erd,edf->erf", inputs, expert_gate, preferred_element_type=F32)
    upper = jnp.einsum("erd,edf->erf", inputs, expert_up, preferred_element_type=F32)
    act = (jax.nn.silu(gate) * upper).astype(BF16)
    result = jnp.einsum("erf,efd->erd", act, expert_down, preferred_element_type=F32)
    result = (
        result.astype(BF16)
        .reshape(held, n, capacity, D)
        .transpose(1, 0, 2, 3)
        .reshape(n * held, capacity, D)
    )
    returned = lax.all_to_all(result, "ctx", split_axis=0, concat_axis=0, tiled=True)
    returned = returned.reshape(experts_all * capacity, D)
    picked = jnp.take(returned, target, axis=0).reshape(tokens_here, TOP, D)
    blended = jnp.sum(combine[:, :, None] * picked.astype(F32), axis=1)
    return (hidden.astype(BF16), (hidden + blended).astype(BF16))


def capacity_of(tokens, experts):
    return max(2, 5 * tokens * TOP // (4 * experts))


def solution(mesh):
    n = mesh.shape["ctx"]

    def body(*args):
        tokens, held = args[0].shape[0], args[9].shape[0]
        dense = tokens <= 2 * capacity_of(tokens, held * n) and held == 1
        fits = n >= 16 and n & (n - 1) == 0
        return (ring_body if dense and fits else exchange_body)(n, *args)

    in_specs = (
        P(("groups", "ctx"), None),
        P(("groups", "ctx"), None),
        P(("groups", "ctx"), None),
        P(("groups", "ctx")),
        P("ctx", None),
        P(),
        P(),
        P(("groups", "ctx"), None),
        P(("groups", "ctx"), None),
        P("ctx", None, None),
        P("ctx", None, None),
        P("ctx", None, None),
    )
    out_specs = (P(("groups", "ctx"), None), P(("groups", "ctx"), None))
    return jax.shard_map(body, mesh=mesh, in_specs=in_specs, out_specs=out_specs, check_vma=False)
```
